32 devices in a mesh: expert: 4 (over y, x), head: 8 (over z, core).
Axes of the slice: x: 2, y: 2, z: 4, core: 2. Of those that a mesh axis runs over, the one named last changes fastest.
Arguments:
- table_cells: bfloat16 [2048, 2, 2048], P(('expert', 'head')), may hold values from -8 to 8
- w_query: bfloat16 [2048, 2048], P(None, 'head')
- w_key: bfloat16 [2048, 2048], P(None, 'head')
- w_value: bfloat16 [2048, 2048], P(None, 'head'), may hold values from -0.125 to 0.125
- w_out: bfloat16 [2048, 2048], P('head'), may hold values from -0.125 to 0.125
- norm_gain: bfloat16 [2048], replicated, may hold values from 0.099609375 to 1.8984375
- w_gate: bfloat16 [32, 704, 2048], P(('expert', 'head')), may hold values from -0.125 to 0.125
- w_up: bfloat16 [32, 704, 2048], P(('expert', 'head')), may hold values from -0.125 to 0.125
- w_down: bfloat16 [32, 704, 2048], P(('expert', 'head')), may hold values from -0.15625 to 0.15625
- lengths: int32 [2], replicated, may hold values from 512 to 2048, as said below
- expert_of_cell: int32 [2048, 2], P(('expert', 'head')), may hold values from 0 to 15, as said below
- slot_of_cell: int32 [2048, 2], P(('expert', 'head')), may hold values from 0 to 15, as said below
Outputs:
- updated_cells: bfloat16 [2048, 2, 2048], P(('expert', 'head'))
The draws below stay inside these ranges and needn't reach their ends.
Inputs may be any that keep to these rules, and one draw needn't show every extreme that they name: `lengths`: one table in every draw has all 2048 cells. `expert_of_cell`: within the 128 cells of one device (aligned blocks in row-major order), no expert has more than 16 cells, and in every draw one expert has exactly 16 cells in every device's block. `slot_of_cell`: cells of one device with the same expert have distinct slots.
All inputs are finite; a program needn't handle non-finite values.
Results may differ from the reference program's by a relative error of at most 0.014.
Values may be sent and summed in bfloat16 or wider, within the bound.
No kernel may reach another device: no remote copies, remote signals or barrier semaphores. Data moves between devices by JAX's collectives and lax.ppermute only.
A program may use at most 128 MiB of HBM per device.

```python
import math
import jax
import jax.numpy as jnp
from jax import lax

D = 2048
HEADS = 16
DH = 128
FF = 1408
CELLS_DEV = 64
SEQS = 2
BLOCKS = 32
EXPERTS = 16
CAP = 16
HALF = 704
LENGTH = 2048
N_HEAD = 8


def draw_table_cells(key, part):
    base_key = jax.random.fold_in(key, 3)
    first_key = jax.random.fold_in(base_key, 0)
    shape = (LENGTH, SEQS, D)
    drawn = jnp.clip(jax.random.normal(first_key, shape, jnp.float32), -6.0, 6.0)
    return drawn.astype(jnp.bfloat16)


def attention_pair(key):
    base_key = jax.random.fold_in(key, 11)
    first_key, second_key = jax.random.split(base_key)
    shape = (D, HEADS * DH)
    spread = 1.6 / math.sqrt(D)
    first = jax.random.normal(first_key, shape, jnp.float32) * spread
    second = jax.random.normal(second_key, shape, jnp.float32) * spread
    return (first, second)


def draw_w_query(key, part):
    return attention_pair(key)[0].astype(jnp.bfloat16)


def draw_w_key(key, part):
    return attention_pair(key)[1].astype(jnp.bfloat16)


def draw_lengths(key, part):
    base_key = jax.random.fold_in(key, 5)
    first_key, second_key = jax.random.split(base_key)
    drawn_lengths = jax.random.randint(first_key, (SEQS,), LENGTH // 4, LENGTH + 1)
    full_table = jax.random.randint(second_key, (), 0, SEQS)
    return jnp.where(jnp.arange(SEQS, dtype=jnp.int32) == full_table, LENGTH, drawn_lengths).astype(jnp.int32)


def routing(key):
    base_key = jax.random.fold_in(key, 23)
    hot_key, block_key = jax.random.split(base_key)
    hot_expert = jax.random.randint(hot_key, (), 0, EXPERTS)
    block_keys = jax.random.split(block_key, BLOCKS)
    cell_index = jnp.arange(EXPERTS * CAP, dtype=jnp.int32).reshape(EXPERTS, CAP)

    def one_block(single_key):
        level_key, jitter_key, order_key = jax.random.split(single_key, 3)
        levels = jax.random.randint(level_key, (EXPERTS,), 0, 4)
        levels = jnp.where(jnp.arange(EXPERTS, dtype=jnp.int32) == hot_expert, 8, levels)
        jitter = jax.random.randint(jitter_key, (EXPERTS, CAP), 0, 1024)
        ranking = ((levels[:, None] * 1024 + jitter) * (EXPERTS * CAP) + cell_index).reshape(-1)
        chosen = lax.top_k(ranking, CELLS_DEV * SEQS)[1]
        chosen = chosen[jax.random.permutation(order_key, CELLS_DEV * SEQS)]
        return (chosen // CAP, chosen % CAP)
    experts_drawn, slots_drawn = jax.vmap(one_block)(block_keys)
    return (experts_drawn.reshape(LENGTH, SEQS).astype(jnp.int32), slots_drawn.reshape(LENGTH, SEQS).astype(jnp.int32))


def draw_expert_of_cell(key, part):
    return routing(key)[0]


def draw_slot_of_cell(key, part):
    return routing(key)[1]


def steps_of(rng, dims, shards, low, top_value):
    level = 1.0
    for dim, shards_of in shards:
        heights = jax.random.uniform(jax.random.fold_in(jax.random.fold_in(rng, 6), dim), (shards_of,), jnp.float32, low / len(shards), top_value / len(shards))
        level = level * jnp.repeat(jnp.exp(heights), dims[dim] // shards_of).reshape((-1,) + (1,) * (len(dims) - 1 - dim))
    return level


def centred(rng, dims, scale, most, cuts=(), held_as=jnp.bfloat16):
    array = jax.random.normal(rng, dims, jnp.float32) * scale
    if len(cuts) > 0:
        array = steps_of(rng, dims, cuts, -0.22, 0.18) * array
    return jnp.clip(array, min=-most, max=most).astype(held_as)


def setup_inputs(seed: int = 0) -> dict:
    streams_of = jax.random.split(jax.random.key(seed), 13)
    table_cells = draw_table_cells(jax.random.fold_in(streams_of[12], 71), 0)
    w_query = draw_w_query(jax.random.fold_in(streams_of[12], 71), 0)
    w_key = draw_w_key(jax.random.fold_in(streams_of[12], 71), 0)
    w_value = centred(streams_of[3], (D, HEADS * DH), D ** -0.5, 0.125, ((1, 8),))
    w_out = centred(streams_of[4], (HEADS * DH, D), (HEADS * DH) ** -0.5, 0.125, ((0, 8),))
    norm_gain = jnp.clip(1.0 + 0.18 * jax.random.normal(streams_of[5], (D,), jnp.float32), 0.099609375, 1.8984375).astype(jnp.bfloat16)
    w_gate = centred(streams_of[6], (2 * EXPERTS, HALF, D), D ** -0.5, 0.125, ((0, 32),))
    w_up = centred(streams_of[7], (2 * EXPERTS, HALF, D), D ** -0.5, 0.125, ((0, 32),))
    w_down = centred(streams_of[8], (2 * EXPERTS, HALF, D), FF ** -0.5, 0.15625, ((0, 32),))
    lengths = draw_lengths(jax.random.fold_in(streams_of[12], 71), 0)
    expert_of_cell = draw_expert_of_cell(jax.random.fold_in(streams_of[12], 71), 0)
    slot_of_cell = draw_slot_of_cell(jax.random.fold_in(streams_of[12], 71), 0)
    return dict(table_cells=table_cells, w_query=w_query, w_key=w_key, w_value=w_value, w_out=w_out, norm_gain=norm_gain, w_gate=w_gate, w_up=w_up, w_down=w_down, lengths=lengths, expert_of_cell=expert_of_cell, slot_of_cell=slot_of_cell)


def attend_head(query_head, key_head, value_head, length):
    scores = jnp.dot(query_head, key_head.T, preferred_element_type=jnp.float32) * (1.0 / math.sqrt(DH))
    position = jnp.arange(query_head.shape[0], dtype=jnp.int32)
    scores = jnp.where(position[None, :] < length, scores, -jnp.inf)
    row_top = lax.optimization_barrier(jnp.max(scores, axis=-1, keepdims=True))
    exp_scores = jnp.exp(scores - row_top)
    denominator = lax.optimization_barrier(jnp.sum(exp_scores, axis=-1, keepdims=True))
    result = jnp.dot(exp_scores.astype(jnp.bfloat16), value_head, preferred_element_type=jnp.float32) / denominator
    result = jnp.where(position[:, None] < length, result, 0.0)
    return result.astype(jnp.bfloat16)

def run_expert(group_item):
    slot_rows, gate_pair, up_pair, down_pair = group_item
    summed = jnp.zeros((slot_rows.shape[0], D), jnp.float32)
    for half_index in range(2):
        gate_t = jnp.dot(gate_pair[half_index], slot_rows.T, preferred_element_type=jnp.float32)
        up_t = jnp.dot(up_pair[half_index], slot_rows.T, preferred_element_type=jnp.float32)
        hidden = (jax.nn.silu(gate_t) * up_t).astype(jnp.bfloat16)
        partial_value = jnp.dot(hidden.T, down_pair[half_index], preferred_element_type=jnp.float32).astype(jnp.bfloat16)
        summed = summed + partial_value.astype(jnp.float32)
    return summed.astype(jnp.bfloat16)

def reference(table_cells, w_query, w_key, w_value, w_out, norm_gain, w_gate, w_up, w_down, lengths, expert_of_cell, slot_of_cell):
    flat_cells = table_cells.reshape(LENGTH * SEQS, D)

    def heads_of(weight):
        projected = jnp.dot(flat_cells, weight, preferred_element_type=jnp.float32).astype(jnp.bfloat16)
        projected = projected.reshape(LENGTH, SEQS, HEADS, DH).transpose(1, 2, 0, 3)
        return projected.reshape(SEQS * HEADS, LENGTH, DH)
    queries = heads_of(w_query)
    key_rows = heads_of(w_key)
    value_rows = heads_of(w_value)
    length_rows = jnp.repeat(lengths, HEADS)
    attended = lax.map(lambda group_item: attend_head(*group_item), (queries, key_rows, value_rows, length_rows))
    attended = attended.reshape(SEQS, HEADS, LENGTH, DH).transpose(2, 0, 1, 3).reshape(LENGTH * SEQS, HEADS * DH)
    group_width = HEADS // N_HEAD * DH
    summed = jnp.zeros((LENGTH * SEQS, D), jnp.float32)
    for group_index in range(N_HEAD):
        lower = group_index * group_width
        partial_value = jnp.dot(attended[:, lower:lower + group_width], w_out[lower:lower + group_width], preferred_element_type=jnp.float32).astype(jnp.bfloat16)
        summed = summed + partial_value.astype(jnp.float32)
    residual = flat_cells.astype(jnp.float32) + summed
    mean_square = lax.optimization_barrier(jnp.mean(residual * residual, axis=-1, keepdims=True))
    normed = (residual * lax.rsqrt(mean_square + 1e-06) * norm_gain.astype(jnp.float32)).astype(jnp.bfloat16)
    device_of = jnp.arange(LENGTH * SEQS, dtype=jnp.int32) // (CELLS_DEV * SEQS)
    slot_place = device_of * (EXPERTS * CAP) + expert_of_cell.reshape(-1).astype(jnp.int32) * CAP + slot_of_cell.reshape(-1).astype(jnp.int32)
    buffer = jnp.zeros((BLOCKS * EXPERTS * CAP, D), jnp.bfloat16).at[slot_place].add(normed)
    buffer = buffer.reshape(BLOCKS, EXPERTS, CAP, D).transpose(1, 0, 2, 3).reshape(EXPERTS, BLOCKS * CAP, D)
    gate_pairs = w_gate.reshape(EXPERTS, 2, FF // 2, D)
    up_pairs = w_up.reshape(EXPERTS, 2, FF // 2, D)
    down_pairs = w_down.reshape(EXPERTS, 2, FF // 2, D)
    results = lax.map(run_expert, (buffer, gate_pairs, up_pairs, down_pairs))
    results = results.reshape(EXPERTS, BLOCKS, CAP, D).transpose(1, 0, 2, 3).reshape(BLOCKS * EXPERTS * CAP, D)
    expert_out = results[slot_place]
    updated = (residual + expert_out.astype(jnp.float32)).astype(jnp.bfloat16)
    return updated.reshape(LENGTH, SEQS, D)
```

```python
import functools
import math

import jax
import jax.numpy as jnp
from jax import lax
from jax.experimental import pallas as pl
from jax.experimental.pallas import tpu as pltpu
from jax.sharding import PartitionSpec as P

DH = 128
VMEM = pl.BlockSpec(memory_space=pltpu.VMEM)
SMEM = pl.BlockSpec(memory_space=pltpu.SMEM)
ROWS_BY_ROWS = (((1,), (1,)), ((), ()))
GRANT = 56 * 1024 * 1024


def local_call(body, outs, args, specs, flops, scratch=()):
    moved = sum(a.size * a.dtype.itemsize for a in list(args) + list(outs))
    return pl.pallas_call(
        body,
        out_shape=outs,
        in_specs=specs,
        out_specs=[VMEM] * len(outs),
        scratch_shapes=list(scratch),
        compiler_params=pltpu.CompilerParams(vmem_limit_bytes=GRANT),
        cost_estimate=pl.CostEstimate(flops=flops, bytes_accessed=moved, transcendentals=0),
    )(*args)


def shape_of(dims, dtype=jnp.bfloat16):
    return jax.ShapeDtypeStruct(dims, dtype)


def swap_cores(block):
    count = lax.axis_size("head")
    return lax.ppermute(block, "head", [(h, h ^ 1) for h in range(count)])


def along_z(block, step, first):
    planes = lax.axis_size("head") // 2
    route = []
    for z in range(planes):
        there = z + step
        behind = z if step > 0 else planes - 1 - z
        if 0 <= there < planes and behind >= first:
            route += [(2 * z + core, 2 * there + core) for core in range(2)]
    return lax.ppermute(block, "head", route)


def round_z(block, step):
    count = lax.axis_size("head")
    return lax.ppermute(block, "head", [(h, (h - 2 * step) % count) for h in range(count)])


def in_plane(block, bits):
    count = lax.axis_size("expert")
    return lax.ppermute(block, "expert", [(e, e ^ bits) for e in range(count)])


def in_plane_and_core(block, bits, core_bit):
    heads = lax.axis_size("head")
    count = lax.axis_size("expert") * heads
    route = [(d, ((d // heads) ^ bits) * heads + ((d % heads) ^ core_bit)) for d in range(count)]
    return lax.ppermute(block, ("expert", "head"), route)


def project_body(pieces, half, *refs):
    inputs, weight_ref, outs = refs[: 4 * pieces], refs[4 * pieces], refs[4 * pieces + 1 :]
    width = weight_ref.shape[1] // 2
    for table in range(2):
        for piece in range(pieces):
            first, second = inputs[4 * piece + 2 * table : 4 * piece + 2 * table + 2]
            rows = jnp.concatenate([first[...], second[...]], axis=0)
            mixed = jnp.dot(rows, weight_ref[...], preferred_element_type=jnp.float32)
            mixed = mixed.astype(jnp.bfloat16)
            span = pl.ds(piece * 2 * half, 2 * half)
            outs[2 * table][span, :] = mixed[:, :width]
            outs[2 * table + 1][span, :] = mixed[:, width:]


def project(groups, weight):
    pieces, half, width = len(groups), groups[0][0].shape[0], weight.shape[1] // 2
    args = [block for group in groups for block in group] + [weight]
    outs = [shape_of((pieces * 2 * half, width))] * 4
    return local_call(
        functools.partial(project_body, pieces, half),
        outs,
        args,
        [VMEM] * len(args),
        2 * pieces * 4 * half * weight.size,
    )


def attend_body(block, place_ref, bias_ref, *refs):
    sources = 4
    early, middle, late = refs[:4], refs[4:8], refs[8:12]
    outs, (queries, keys, values) = refs[12:16], refs[16:19]
    place = place_ref[0]
    for source in range(sources):
        last = late[source][...]
        near = early[source][pl.ds(block, block), :]
        far = early[source][pl.ds(2 * block, block), :]
        rows = (
            early[source][pl.ds(0, block), :],
            jnp.where(place == 0, last, near),
            middle[source][...],
            jnp.where(place == 3, last, far),
        )
        for offset in range(4):
            key_span = pl.ds((offset * sources + source) * block, block)
            queries[key_span, :] = rows[offset][:, :DH]
            keys[key_span, :] = rows[offset][:, DH : 2 * DH]
            values[key_span, :] = rows[offset][:, 2 * DH :]
    scale = 1.0 / math.sqrt(DH) * math.log2(math.e)
    chunk = 256
    per_out = sources * block // chunk
    for step in range(4 * per_out):
        scores = lax.dot_general(
            queries[pl.ds(step * chunk, chunk), :],
            keys[...],
            ROWS_BY_ROWS,
            preferred_element_type=jnp.float32,
        )
        scores = scores + bias_ref[...]
        top = jnp.max(scores, axis=1, keepdims=True)
        weights = jnp.exp2((scores - top) * scale)
        total = jnp.sum(weights, axis=1, keepdims=True)
        mixed = jnp.dot(
            weights.astype(jnp.bfloat16), values[...], preferred_element_type=jnp.float32
        )
        outs[step // per_out][pl.ds(step % per_out * chunk, chunk), :] = (mixed / total).astype(
            jnp.bfloat16
        )


def regroup_body(block, *refs):
    for offset in range(4):
        for target in range(8):
            refs[4 + target][pl.ds(offset * block, block), :] = refs[offset][
                pl.ds(target * block, block), :
            ]


def join_body(planes, place_ref, own_ref, live_ref, target_ref, gain_ref, *refs):
    pieces, out_weight = refs[:8], refs[8]
    residual_ref, send_ref, joined = refs[9:]
    place, core, parity = place_ref[0], place_ref[1], place_ref[2]
    block = joined.shape[0] // 2
    for source in range(4):
        table, head_bit = source >> 1, source & 1
        for core_bit in range(2):
            piece = pieces[2 * source + core_bit]
            for offset in range(planes):
                device = 2 * lax.rem(place + offset, planes) + (core ^ core_bit)
                head = 2 * device + (parity ^ head_bit)
                columns = pl.ds(pl.multiple_of(head * DH, DH), DH)
                joined[pl.ds(table * block, block), columns] = piece[
                    pl.ds(offset * block, block), :
                ]
    attended = jnp.where(live_ref[...] > 0, joined[...].astype(jnp.float32), 0.0)
    summed = jnp.dot(
        attended.astype(jnp.bfloat16), out_weight[...], preferred_element_type=jnp.float32
    )
    residual = own_ref[...].astype(jnp.float32) + summed
    residual_ref[...] = residual
    mean_square = jnp.mean(residual * residual, axis=1, keepdims=True)
    normed = residual * lax.rsqrt(mean_square + 1e-06) * gain_ref[...].astype(jnp.float32)
    slots = send_ref.shape[0]
    table = lax.broadcasted_iota(jnp.int32, (slots, joined.shape[0]), 0) == target_ref[...]
    send_ref[...] = jnp.dot(
        table.astype(jnp.float32).astype(jnp.bfloat16),
        normed.astype(jnp.bfloat16),
        preferred_element_type=jnp.float32,
    ).astype(jnp.bfloat16)


def expert_body(own_ref, other_ref, gate_ref, up_ref, down_ref, own_out, other_out):
    for rows_ref, out_ref in ((other_ref, other_out), (own_ref, own_out)):
        rows = rows_ref[...]
        gate = lax.dot_general(
            rows, gate_ref[...], ROWS_BY_ROWS, preferred_element_type=jnp.float32
        )
        up = lax.dot_general(rows, up_ref[...], ROWS_BY_ROWS, preferred_element_type=jnp.float32)
        hidden = (gate / (1.0 + jnp.exp(-gate)) * up).astype(jnp.bfloat16)
        out_ref[...] = jnp.dot(
            hidden, down_ref[...], preferred_element_type=jnp.float32
        ).astype(jnp.bfloat16)


def paired_shards(
    table_cells,
    w_query,
    w_key,
    w_value,
    w_out,
    norm_gain,
    w_gate,
    w_up,
    w_down,
    lengths,
    expert_of_cell,
    slot_of_cell,
):
    cells, tables, width = table_cells.shape
    heads = lax.axis_size("head")
    planes = heads // 2
    spot, place_head = lax.axis_index("expert"), lax.axis_index("head")
    mine, parity = spot // 2, spot % 2
    place, core = place_head // 2, place_head % 2

    by_table = jnp.transpose(table_cells, (1, 0, 2))
    by_table = jnp.where(mine == 0, by_table, by_table[::-1])
    own = [by_table[0], by_table[1]]

    def columns(which):
        return [
            lax.dynamic_slice_in_dim(w, which * DH, DH, 1) for w in (w_query, w_key, w_value)
        ]

    weight = jnp.concatenate(columns(parity) + columns(1 - parity), axis=1)

    up = [[block] for block in own]
    down = [[block] for block in own]
    for stage in range(planes - 1):
        for table in range(2):
            up[table].append(along_z(up[table][stage], 1, stage))
            down[table].append(along_z(down[table][stage], -1, stage))

    def with_other(blocks):
        return [part for block in blocks for part in (block, swap_cores(block))]

    later = [jnp.where(place < 2, down[t][2], up[t][2]) for t in range(2)]
    last = [jnp.where(place < 2, down[t][3], up[t][3]) for t in range(2)]
    early_out = project(
        [
            with_other(own),
            with_other([up[0][1], up[1][1]]),
            with_other([down[0][1], down[1][1]]),
        ],
        weight,
    )
    middle_out = project([with_other(later)], weight)
    late_out = project([with_other(last)], weight)

    def spread(outs):
        return [outs[0]] + [in_plane(outs[bits], bits) for bits in range(1, 4)]

    shared = spread(early_out) + spread(middle_out) + spread(late_out)

    block = 2 * cells
    offsets = jnp.arange(planes, dtype=jnp.int32)[:, None, None, None]
    sources = jnp.arange(4, dtype=jnp.int32)[None, :, None, None]
    sides = jnp.arange(2, dtype=jnp.int32)[None, None, :, None]
    inner = jnp.arange(cells, dtype=jnp.int32)[None, None, None, :]
    device = (spot ^ sources) * heads + 2 * ((place - offsets) % planes) + (core ^ sides)
    positions = (device * cells + inner).reshape(1, planes * 4 * block)
    bias = jnp.where(positions < lengths[mine], 0.0, -jnp.inf).astype(jnp.float32)
    count = planes * 4 * block
    attended = local_call(
        functools.partial(attend_body, block),
        [shape_of((4 * block, DH))] * 4,
        [place.reshape(1).astype(jnp.int32), bias] + shared,
        [SMEM] + [VMEM] * 13,
        4 * count * count * DH,
        [pltpu.VMEM((count, DH), jnp.bfloat16)] * 3,
    )
    arrived = [attended[0]] + [round_z(attended[k], k) for k in range(1, planes)]
    grouped = local_call(
        functools.partial(regroup_body, cells),
        [shape_of((planes * cells, DH))] * 8,
        arrived,
        [VMEM] * 4,
        0,
    )
    pieces = [grouped[0]] + [
        in_plane_and_core(grouped[i], i >> 1, i & 1) for i in range(1, 8)
    ]

    quarter = w_out.shape[0] // 4
    part = lax.dynamic_slice_in_dim(w_out, spot * quarter, quarter, 0)
    parts = lax.all_gather(part, "head", axis=0, tiled=False)
    whole = lax.all_gather(parts, "expert", axis=1, tiled=False)
    out_weight = whole.reshape(heads * w_out.shape[0], width)

    rows_dev = cells * tables
    own_rows = by_table.reshape(rows_dev, width)
    own_positions = (spot * heads + place_head) * cells + jnp.arange(cells, dtype=jnp.int32)
    table_order = jnp.stack([mine, 1 - mine])
    live = (own_positions[None, :] < lengths[table_order][:, None]).astype(jnp.int32)
    expert_count = lax.axis_size("expert") * heads // 2
    slot_cap = 2 * max(1, rows_dev // expert_count)
    target = expert_of_cell * slot_cap + slot_of_cell
    target = jnp.take(target.T, table_order, axis=0).reshape(1, rows_dev)
    slots = expert_count * slot_cap
    residual, send_rows = local_call(
        functools.partial(join_body, planes),
        [shape_of((rows_dev, width), jnp.float32), shape_of((slots, width))],
        [
            jnp.stack([place, core, parity]).astype(jnp.int32),
            own_rows,
            live.reshape(rows_dev, 1),
            target,
            norm_gain.reshape(1, width),
        ]
        + pieces
        + [out_weight],
        [SMEM] + [VMEM] * 13,
        2 * rows_dev * width * (width + slots),
        [pltpu.VMEM((rows_dev, width), jnp.bfloat16)],
    )

    everyone = ("expert", "head")
    received = lax.all_to_all(
        send_rows.reshape(2 * expert_count, slot_cap // 2, width), everyone, 0, 0, tiled=True
    ).reshape(slots, width)
    other_rows = swap_cores(received)
    own_part, other_part = local_call(
        expert_body,
        [shape_of((slots, width))] * 2,
        [received, other_rows, w_gate[0], w_up[0], w_down[0]],
        [VMEM] * 5,
        2 * 2 * slots * 3 * w_gate.size,
    )
    returned = swap_cores(other_part)
    merged = (own_part.astype(jnp.float32) + returned.astype(jnp.float32)).astype(jnp.bfloat16)
    gathered = lax.all_to_all(
        merged.reshape(2 * expert_count, slot_cap // 2, width), everyone, 0, 0, tiled=True
    ).reshape(slots, width)
    chosen = (jnp.arange(slots, dtype=jnp.int32)[:, None] == target).astype(jnp.bfloat16)
    expert_out = lax.dot_general(
        chosen, gathered, (((0,), (0,)), ((), ())), preferred_element_type=jnp.float32
    )
    updated = (residual + expert_out).astype(jnp.bfloat16).reshape(tables, cells, width)
    updated = jnp.where(mine == 0, updated, updated[::-1])
    return jnp.transpose(updated, (1, 0, 2))


def from_partner(block, axis, bit):
    count = lax.axis_size(axis)
    route = []
    for low in range(count):
        high = low | 1 << bit
        if high != low and high < count:
            route += [(low, high), (high, low)]
    return lax.ppermute(block, axis, route)


def expert_half(slot_rows, gate_half, up_half, down_half):
    contract_rows = (((1,), (1,)), ((), ()))
    gate_t = lax.dot_general(
        gate_half, slot_rows, contract_rows, preferred_element_type=jnp.float32
    )
    up_t = lax.dot_general(up_half, slot_rows, contract_rows, preferred_element_type=jnp.float32)
    hidden = (jax.nn.silu(gate_t) * up_t).astype(jnp.bfloat16)
    product = lax.dot_general(
        hidden, down_half, (((0,), (0,)), ((), ())), preferred_element_type=jnp.float32
    )
    return product.astype(jnp.bfloat16)


def shards(
    table_cells,
    w_query,
    w_key,
    w_value,
    w_out,
    norm_gain,
    w_gate,
    w_up,
    w_down,
    lengths,
    expert_of_cell,
    slot_of_cell,
):
    cell_count, tables, model_width = table_cells.shape
    head_width = w_query.shape[1]
    head_count = head_width // DH
    score_scale = 1.0 / math.sqrt(DH)
    joined = jnp.concatenate([w_query, w_key, w_value], axis=1)
    shard_rows = lax.all_gather(table_cells, "head", axis=0, tiled=True)
    rows_here = shard_rows.shape[0]
    mixed_rows = jnp.dot(
        shard_rows.reshape(rows_here * tables, model_width),
        joined,
        preferred_element_type=jnp.float32,
    )
    projected = mixed_rows.astype(jnp.bfloat16).reshape(rows_here, tables, 3 * head_width)
    row_cells = projected.shape[0]
    queries = projected[:, :, :head_width].reshape(row_cells, tables, head_count, DH)
    key_rows = projected[:, :, head_width : 2 * head_width]
    value_rows = projected[:, :, 2 * head_width :]
    offset = lax.axis_index("expert") * row_cells
    own_positions = offset + jnp.arange(row_cells, dtype=jnp.int32)
    start_state = (
        jnp.full((tables, head_count, row_cells), -1e30, jnp.float32),
        jnp.zeros((tables, head_count, row_cells), jnp.float32),
        jnp.zeros((tables, head_count, row_cells, DH), jnp.float32),
    )
    key_piece = lax.all_gather(key_rows, "expert", axis=0, tiled=True)
    value_piece = lax.all_gather(value_rows, "expert", axis=0, tiled=True)
    piece_len = key_piece.shape[0]
    block_len = math.gcd(piece_len, 512)
    block_count = piece_len // block_len
    key_blocks = key_piece.reshape(block_count, block_len, tables, head_count, DH)
    value_blocks = value_piece.reshape(block_count, block_len, tables, head_count, DH)
    block_starts = jnp.arange(block_count, dtype=jnp.int32) * block_len

    def step(carried, block_item):
        running_max, running_sum, accum = carried
        key_block, value_block, block_first = block_item
        scores = (
            jnp.einsum("qshd,kshd->shqk", queries, key_block, preferred_element_type=jnp.float32)
            * score_scale
        )
        key_valid = (block_first + jnp.arange(block_len, dtype=jnp.int32))[None, :] < lengths[
            :, None
        ]
        scores = jnp.where(key_valid[:, None, None, :], scores, -jnp.inf)
        new_max = jnp.maximum(running_max, jnp.max(scores, axis=-1))
        factor = jnp.exp(running_max - new_max)
        exp_scores = jnp.exp(scores - new_max[..., None])
        running_sum = running_sum * factor + jnp.sum(exp_scores, axis=-1)
        accum = accum * factor[..., None] + jnp.einsum(
            "shqk,kshd->shqd",
            exp_scores.astype(jnp.bfloat16),
            value_block,
            preferred_element_type=jnp.float32,
        )
        return ((new_max, running_sum, accum), None)

    finished, _ = lax.scan(step, start_state, (key_blocks, value_blocks, block_starts))
    running_max, running_sum, accum = finished
    normalized = accum / running_sum[..., None]
    live = own_positions[None, :] < lengths[:, None]
    normalized = jnp.where(live[:, None, :, None], normalized, 0.0)
    attended = (
        jnp.transpose(normalized, (2, 0, 1, 3))
        .reshape(row_cells, tables, head_width)
        .astype(jnp.bfloat16)
    )
    count_rows = cell_count * lax.axis_size("head")
    product = jnp.dot(
        attended.reshape(count_rows * tables, head_width), w_out, preferred_element_type=jnp.float32
    )
    summed = lax.psum_scatter(
        product.reshape(count_rows, tables, model_width).astype(jnp.bfloat16),
        "head",
        scatter_dimension=0,
        tiled=True,
    ).astype(jnp.float32)
    residual = table_cells.astype(jnp.float32) + summed
    mean_square = jnp.mean(residual * residual, axis=-1, keepdims=True)
    normed = (residual * lax.rsqrt(mean_square + 1e-06) * norm_gain.astype(jnp.float32)).astype(
        jnp.bfloat16
    )
    rows_dev = cell_count * tables
    normed_rows = normed.reshape(rows_dev, model_width)
    expert_count = lax.axis_size("expert") * lax.axis_size("head") // 2
    slot_cap = 2 * max(1, rows_dev // expert_count)
    target = expert_of_cell.reshape(rows_dev) * slot_cap + slot_of_cell.reshape(rows_dev)
    slot_table = (
        jnp.arange(expert_count * slot_cap, dtype=jnp.int32)[:, None] == target[None, :]
    ).astype(jnp.bfloat16)
    send_rows = jnp.dot(slot_table, normed_rows, preferred_element_type=jnp.float32).astype(
        jnp.bfloat16
    )
    gate_half = w_gate[0]
    up_half = w_up[0]
    down_half = w_down[0]
    split_rows = send_rows.reshape(2 * expert_count, slot_cap // 2, model_width)
    received = lax.all_to_all(
        split_rows, ("expert", "head"), split_axis=0, concat_axis=0, tiled=True
    )
    item_count = received.shape[1]
    partner_rows = from_partner(received, "head", 0)
    apply_received = jnp.concatenate([received, partner_rows], axis=1)
    sources = apply_received.shape[0]
    apply_item_count = apply_received.shape[1]
    flat_rows = apply_received.reshape(sources * apply_item_count, model_width)
    computed = expert_half(flat_rows, gate_half, up_half, down_half).reshape(
        sources, apply_item_count, model_width
    )
    returned = from_partner(computed[:, item_count:], "head", 0)
    merged = (computed[:, :item_count].astype(jnp.float32) + returned.astype(jnp.float32)).astype(
        jnp.bfloat16
    )
    gathered = lax.all_to_all(merged, ("expert", "head"), split_axis=0, concat_axis=0, tiled=True)
    combined = gathered.reshape(expert_count * slot_cap, model_width)
    expert_out = lax.dot_general(
        slot_table, combined, (((0,), (0,)), ((), ())), preferred_element_type=jnp.float32
    )
    updated = (residual.reshape(rows_dev, model_width) + expert_out).astype(jnp.bfloat16)
    return updated.reshape(cell_count, tables, model_width)


def solution(mesh):
    placed = (
        P(("expert", "head"), None, None),
        P(None, "head"),
        P(None, "head"),
        P(None, "head"),
        P("head", None),
        P(),
        P(("expert", "head"), None, None),
        P(("expert", "head"), None, None),
        P(("expert", "head"), None, None),
        P(),
        P(("expert", "head"), None),
        P(("expert", "head"), None),
    )
    pairs = mesh.shape["expert"] == 4 and mesh.shape["head"] == 8
    return jax.shard_map(
        paired_shards if pairs else shards,
        mesh=mesh,
        in_specs=placed,
        out_specs=P(("expert", "head"), None, None),
        check_vma=False,
    )
```

```python
import functools
import math

import jax
import jax.numpy as jnp
from jax import lax
from jax.experimental import pallas as pl
from jax.experimental.pallas import tpu as pltpu
from jax.sharding import PartitionSpec as P

DH = 128
VMEM = pl.BlockSpec(memory_space=pltpu.VMEM)
SMEM = pl.BlockSpec(memory_space=pltpu.SMEM)
ROWS_BY_ROWS = (((1,), (1,)), ((), ()))


def local_call(body, outs, args, specs, flops, scratch=(), grant=60):
    moved = sum(a.size * a.dtype.itemsize for a in list(args) + list(outs))
    return pl.pallas_call(
        body,
        out_shape=outs,
        in_specs=specs,
        out_specs=[VMEM] * len(outs),
        scratch_shapes=list(scratch),
        compiler_params=pltpu.CompilerParams(vmem_limit_bytes=grant * 1024 * 1024),
        cost_estimate=pl.CostEstimate(flops=flops, bytes_accessed=moved, transcendentals=0),
    )(*args)


def shape_of(dims, dtype=jnp.bfloat16):
    return jax.ShapeDtypeStruct(dims, dtype)


def swap_cores(block):
    count = lax.axis_size("head")
    return lax.ppermute(block, "head", [(h, h ^ 1) for h in range(count)])


def neighbours(block, first):
    planes = lax.axis_size("head") // 2
    route = []
    for low in range(first, planes - 1, 2):
        for core in range(2):
            here, there = 2 * low + core, 2 * low + 2 + core
            route += [(here, there), (there, here)]
    return lax.ppermute(block, "head", route)


def outwards(block):
    route = [(2 * a + core, 2 * b + core) for a, b in ((1, 0), (2, 3)) for core in range(2)]
    return lax.ppermute(block, "head", route)


def across_z(block, bits):
    count = lax.axis_size("head")
    return lax.ppermute(block, "head", [(h, h ^ (2 * bits)) for h in range(count)])


def in_plane(block, bits):
    count = lax.axis_size("expert")
    return lax.ppermute(block, "expert", [(e, e ^ bits) for e in range(count)])


def stack_body(*refs):
    half = refs[0].shape[0] // 2
    for index, ref in enumerate(refs[:-2]):
        for side in range(2):
            refs[side - 2][pl.ds(index * half, half), :] = ref[pl.ds(side * half, half), :]


def stack(blocks):
    rows, width = blocks[0].shape
    shape = shape_of((len(blocks) * rows // 2, width))
    return local_call(stack_body, [shape] * 2, blocks, [VMEM] * len(blocks), 0)


def choose_body(place_ref, *refs):
    out_ref = refs[-1]
    for side in range(2):
        start = pl.multiple_of((place_ref[0] ^ side) * DH, DH)
        for index, ref in enumerate(refs[:-1]):
            out_ref[:, pl.ds((3 * side + index) * DH, DH)] = ref[:, pl.ds(start, DH)]


def project_body(pieces, half, *refs):
    inputs, weight_ref, outs = refs[: 2 * pieces], refs[2 * pieces], refs[2 * pieces + 1 :]
    width = weight_ref.shape[1] // 2
    rows = []
    for table in range(2):
        for piece in range(pieces):
            for side in range(2):
                rows.append(inputs[2 * piece + side][pl.ds(table * half, half), :])
    mixed = jnp.dot(
        jnp.concatenate(rows, axis=0), weight_ref[...], preferred_element_type=jnp.float32
    ).astype(jnp.bfloat16)
    count = pieces * 2 * half
    for table in range(2):
        for side in range(2):
            outs[2 * table + side][...] = mixed[
                table * count : (table + 1) * count, side * width : (side + 1) * width
            ]


def project(blocks, weight):
    pieces, half, width = len(blocks), blocks[0][0].shape[0] // 2, weight.shape[1] // 2
    args = [block for pair in blocks for block in pair] + [weight]
    return local_call(
        functools.partial(project_body, pieces, half),
        [shape_of((pieces * 2 * half, width))] * 4,
        args,
        [VMEM] * len(args),
        2 * pieces * 4 * half * weight.size,
        grant=20,
    )


def attend_body(block, place_ref, bias_ref, *refs):
    early, middle, late = refs[:4], refs[4:8], refs[8:12]
    out_ref, (keys, values) = refs[12], refs[13:]
    spot, place, core = place_ref[0], place_ref[1], place_ref[2]
    planes = 4
    half = block // 2
    for source in range(4):
        parts = (
            early[source][pl.ds(0, block), :],
            early[source][pl.ds(block, block), :],
            middle[source][...],
            late[source][...],
        )
        for slot in range(planes):
            span = pl.ds((slot * 4 + source) * block, block)
            keys[span, :] = parts[slot][:, DH : 2 * DH]
            values[span, :] = parts[slot][:, 2 * DH :]
    scale = 1.0 / math.sqrt(DH) * math.log2(math.e)
    third = jnp.where(place < 2, 2, 1)
    fourth = jnp.where(place < 2, 3, 0)

    def queries(slot, source):
        if slot < 2:
            return early[source][pl.ds(slot * block, block), pl.ds(0, DH)]
        return (middle, late)[slot - 2][source][:, pl.ds(0, DH)]

    for slot, plane in enumerate((place, place ^ 1, third, fourth)):
        for first in (0, 2):
            rows = jnp.concatenate([queries(slot, first), queries(slot, first + 1)], axis=0)
            scores = lax.dot_general(
                rows, keys[...], ROWS_BY_ROWS, preferred_element_type=jnp.float32
            )
            scores = scores + bias_ref[...]
            top = jnp.max(scores, axis=1, keepdims=True)
            weights = jnp.exp2((scores - top) * scale)
            total = jnp.sum(weights, axis=1, keepdims=True)
            mixed = jnp.dot(
                weights.astype(jnp.bfloat16), values[...], preferred_element_type=jnp.float32
            )
            mixed = (mixed / total).astype(jnp.bfloat16)
            for index in range(4):
                source, side = first + index // 2, index % 2
                device = (spot ^ source) * 2 * planes + 2 * plane + (core ^ side)
                start = pl.multiple_of(device * half, half)
                out_ref[pl.ds(start, half), :] = mixed[index * half : (index + 1) * half]


def join_body(planes, place_ref, own_ref, live_ref, target_ref, gain_ref, heads_ref, *refs):
    weights = (refs[:9], refs[9:18])
    residual_ref, send_ref, joined = refs[18:]
    spot, place, core = place_ref[0], place_ref[1], place_ref[2]
    mine = spot // 2
    block, quarter = joined.shape[0] // 2, weights[0][1].shape[1]
    pair = 2 * DH
    for source in range(4):
        rows = pl.ds(pl.multiple_of((source // 2 ^ mine) * block, block), block)
        for head in range(2 * planes):
            columns = pl.ds(head * pair + source % 2 * DH, DH)
            joined[rows, columns] = heads_ref[
                pl.ds((source * 2 * planes + head) * block, block), :
            ]
    joined[...] = jnp.where(live_ref[...] > 0, joined[...].astype(jnp.float32), 0.0).astype(
        jnp.bfloat16
    )
    squares = jnp.zeros((2 * block, 1), jnp.float32)
    for bits in range(4):
        columns = pl.ds(pl.multiple_of((spot ^ bits) * quarter, quarter), quarter)
        total = own_ref[:, columns].astype(jnp.float32)
        for side in range(2):
            for offset in range(planes):
                device = 2 * (place ^ offset) + (core ^ side)
                start = pl.multiple_of(device * pair, pair)
                if offset == 0:
                    total += jnp.dot(
                        joined[:, pl.ds(start, pair)],
                        weights[side][0][:, columns],
                        preferred_element_type=jnp.float32,
                    )
                    continue
                for half in range(2):
                    total += jnp.dot(
                        joined[:, pl.ds(start + half * DH, DH)],
                        weights[side][1 + 2 * bits + half][pl.ds((offset - 1) * DH, DH), :],
                        preferred_element_type=jnp.float32,
                    )
        residual_ref[:, columns] = total
        squares += jnp.sum(total * total, axis=1, keepdims=True)
    residual = residual_ref[...]
    mean_square = squares / residual.shape[1]
    normed = residual * lax.rsqrt(mean_square + 1e-06) * gain_ref[...].astype(jnp.float32)
    slots = send_ref.shape[0]
    chosen = lax.broadcasted_iota(jnp.int32, (slots, 2 * block), 0) == target_ref[...]
    send_ref[...] = jnp.dot(
        chosen.astype(jnp.float32).astype(jnp.bfloat16),
        normed.astype(jnp.bfloat16),
        preferred_element_type=jnp.float32,
    ).astype(jnp.bfloat16)


def expert_body(rows_ref, *refs):
    sources, out_ref, held, arrivals = refs[:6], refs[6], refs[7:13], refs[13]
    copies = [
        pltpu.make_async_copy(source, place, arrivals.at[index])
        for index, (source, place) in enumerate(zip(sources, held))
    ]
    for copy in copies:
        copy.start()
    rows = rows_ref[...]
    total = jnp.zeros(rows.shape, jnp.float32)
    for half in range(2):
        gate_ref, up_ref, down_ref = held[3 * half : 3 * half + 3]
        copies[3 * half].wait()
        gate = lax.dot_general(
            rows, gate_ref[...], ROWS_BY_ROWS, preferred_element_type=jnp.float32
        )
        copies[3 * half + 1].wait()
        up = lax.dot_general(rows, up_ref[...], ROWS_BY_ROWS, preferred_element_type=jnp.float32)
        hidden = (gate / (1.0 + jnp.exp(-gate)) * up).astype(jnp.bfloat16)
        copies[3 * half + 2].wait()
        total += jnp.dot(hidden, down_ref[...], preferred_element_type=jnp.float32)
    out_ref[...] = total.astype(jnp.bfloat16)


def finish_body(residual_ref, target_ref, blocks_ref, out_ref):
    slots = blocks_ref.shape[0]
    rows = residual_ref.shape[0]
    chosen = target_ref[...] == lax.broadcasted_iota(jnp.int32, (rows, slots), 1)
    expert_out = jnp.dot(
        chosen.astype(jnp.float32).astype(jnp.bfloat16),
        blocks_ref[...],
        preferred_element_type=jnp.float32,
    )
    out_ref[...] = (residual_ref[...] + expert_out).astype(jnp.bfloat16)


def paired_shards(
    table_cells,
    w_query,
    w_key,
    w_value,
    w_out,
    norm_gain,
    w_gate,
    w_up,
    w_down,
    lengths,
    expert_of_cell,
    slot_of_cell,
):
    cells, tables, width = table_cells.shape
    heads = lax.axis_size("head")
    planes = heads // 2
    spot, place_head = lax.axis_index("expert"), lax.axis_index("head")
    mine, parity = spot // 2, spot % 2
    place, core = place_head // 2, place_head % 2

    rows_dev = cells * tables
    first, second = table_cells[:, 0], table_cells[:, 1]
    own = jnp.where(
        mine == 0,
        jnp.concatenate([first, second], axis=0),
        jnp.concatenate([second, first], axis=0),
    )

    weight = pl.pallas_call(
        choose_body,
        out_shape=pltpu.VMEM((width, 6 * DH), w_query.dtype),
        in_specs=[SMEM] + [VMEM] * 3,
        out_specs=VMEM,
        compiler_params=pltpu.CompilerParams(vmem_limit_bytes=56 * 1024 * 1024),
    )(parity.reshape(1).astype(jnp.int32), w_query, w_key, w_value)

    def spread(outs):
        return [outs[0]] + [in_plane(outs[bits], bits) for bits in range(1, 4)]

    block = 2 * cells
    low = place < 2
    held = jnp.stack([place, place ^ 1, jnp.where(low, 2, 1), jnp.where(low, 3, 0)])
    sources = jnp.arange(4, dtype=jnp.int32)[None, :, None, None]
    sides = jnp.arange(2, dtype=jnp.int32)[None, None, :, None]
    cell = jnp.arange(cells, dtype=jnp.int32)[None, None, None, :]
    device = (spot ^ sources) * heads + 2 * held[:, None, None, None] + (core ^ sides)
    count = planes * 4 * block
    positions = (device * cells + cell).reshape(1, count)
    bias = jnp.where(positions < lengths[mine], 0.0, -jnp.inf).astype(jnp.float32)
    where = jnp.stack([spot, place, core]).astype(jnp.int32)
    own_positions = (spot * heads + place_head) * cells + jnp.arange(cells, dtype=jnp.int32)
    table_order = jnp.stack([mine, 1 - mine])
    live = (own_positions[None, :] < lengths[table_order][:, None]).astype(jnp.int32)
    expert_count = lax.axis_size("expert") * heads // 2
    slot_cap = 2 * max(1, rows_dev // expert_count)
    target = (expert_of_cell * slot_cap + slot_of_cell).T
    target = jnp.where(mine == 0, target, target[::-1]).reshape(1, rows_dev)
    slots = expert_count * slot_cap
    live, target, target_column = live.reshape(rows_dev, 1), target, target.reshape(rows_dev, 1)
    gain = norm_gain.reshape(1, width)

    inside = (place == 1) | (place == 2)
    beside = neighbours(own, 0)
    inner = neighbours(own, 1)
    beside_too = swap_cores(beside)
    outer = outwards(inner)
    inner_far = neighbours(beside, 1)
    quarter = width // 4
    part = lax.dynamic_slice_in_dim(w_out, spot * quarter, quarter, 1)
    parts = [across_z(part, bits) for bits in range(1, planes)]
    small = (bias, where, live, target, target_column, gain)
    halves = [w_gate[0], w_up[0], w_down[0]]
    others = [swap_cores(w) for w in halves]
    inner_far, small, weight, others[0] = lax.optimization_barrier(
        (inner_far, small, weight, others[0])
    )
    bias, where, live, target, target_column, gain = small
    early_out = project([(own, swap_cores(own)), (beside, beside_too)], weight)
    early = spread(early_out)
    outer_far = outwards(inner_far)
    third = jnp.where(inside, inner, outer)
    middle_out = project([(third, swap_cores(third))], weight)
    outer_far, middle_out, early, parts[0], parts[1], others[1] = lax.optimization_barrier(
        (outer_far, middle_out, early, parts[0], parts[1], others[1])
    )
    middle = spread(middle_out)
    fourth = jnp.where(inside, inner_far, outer_far)
    late_out = project([(fourth, swap_cores(fourth))], weight)
    late_out, middle = lax.optimization_barrier((late_out, middle))
    late = spread(late_out)

    parts, late, others[2] = lax.optimization_barrier((parts, late, others[2]))
    expert_weights = halves + others
    far = stack(parts)
    far, late = lax.optimization_barrier((far, late))
    shared = early + middle + late
    fars = [[in_plane(half, bits) for half in far] for bits in (1, 2)]
    everyone = ("expert", "head")
    attended = local_call(
        functools.partial(attend_body, block),
        [shape_of((count, DH))],
        [where, bias] + shared,
        [SMEM] + [VMEM] * 13,
        4 * count * count * DH,
        [pltpu.VMEM((count, DH), jnp.bfloat16)] * 2,
        grant=60,
    )[0]
    fars, _ = lax.optimization_barrier((fars, attended))
    across = [in_plane(fars[1][0], 1), in_plane(fars[0][1], 2)]
    same = [w_out, *far, *fars[0], *fars[1], *across]
    out_weights = same + [swap_cores(w) for w in same]
    arrived = lax.all_to_all(attended, everyone, 0, 0, tiled=True)

    residual, send_rows = local_call(
        functools.partial(join_body, planes),
        [shape_of((rows_dev, width), jnp.float32), shape_of((slots, width))],
        [
            where,
            own,
            live,
            target,
            gain,
            arrived,
        ]
        + out_weights,
        [SMEM] + [VMEM] * 23,
        2 * rows_dev * width * (width + slots),
        [pltpu.VMEM((rows_dev, width), jnp.bfloat16)],
    )

    received = lax.all_to_all(send_rows, everyone, 0, 0, tiled=True)
    computed = local_call(
        expert_body,
        [shape_of((slots, width))],
        [received] + expert_weights,
        [VMEM] + [pl.BlockSpec(memory_space=pl.ANY)] * 6,
        2 * slots * 6 * w_gate.size,
        [pltpu.VMEM(w.shape, w.dtype) for w in expert_weights] + [pltpu.SemaphoreType.DMA((6,))],
        grant=60,
    )[0]
    gathered = lax.all_to_all(computed, everyone, 0, 0, tiled=True)
    updated = local_call(
        finish_body,
        [shape_of((rows_dev, width))],
        [residual, target_column, gathered],
        [VMEM] * 3,
        2 * rows_dev * width * slots,
        grant=60,
    )[0]
    first, second = updated[:cells], updated[cells:]
    return jnp.stack(
        [jnp.where(mine == 0, first, second), jnp.where(mine == 0, second, first)], axis=1
    )


def from_partner(block, axis, bit):
    count = lax.axis_size(axis)
    route = []
    for low in range(count):
        high = low | 1 << bit
        if high != low and high < count:
            route += [(low, high), (high, low)]
    return lax.ppermute(block, axis, route)


def expert_half(slot_rows, gate_half, up_half, down_half):
    contract_rows = (((1,), (1,)), ((), ()))
    gate_t = lax.dot_general(
        gate_half, slot_rows, contract_rows, preferred_element_type=jnp.float32
    )
    up_t = lax.dot_general(up_half, slot_rows, contract_rows, preferred_element_type=jnp.float32)
    hidden = (jax.nn.silu(gate_t) * up_t).astype(jnp.bfloat16)
    product = lax.dot_general(
        hidden, down_half, (((0,), (0,)), ((), ())), preferred_element_type=jnp.float32
    )
    return product.astype(jnp.bfloat16)


def shards(
    table_cells,
    w_query,
    w_key,
    w_value,
    w_out,
    norm_gain,
    w_gate,
    w_up,
    w_down,
    lengths,
    expert_of_cell,
    slot_of_cell,
):
    cell_count, tables, model_width = table_cells.shape
    head_width = w_query.shape[1]
    head_count = head_width // DH
    score_scale = 1.0 / math.sqrt(DH)
    joined = jnp.concatenate([w_query, w_key, w_value], axis=1)
    shard_rows = lax.all_gather(table_cells, "head", axis=0, tiled=True)
    rows_here = shard_rows.shape[0]
    mixed_rows = jnp.dot(
        shard_rows.reshape(rows_here * tables, model_width),
        joined,
        preferred_element_type=jnp.float32,
    )
    projected = mixed_rows.astype(jnp.bfloat16).reshape(rows_here, tables, 3 * head_width)
    row_cells = projected.shape[0]
    queries = projected[:, :, :head_width].reshape(row_cells, tables, head_count, DH)
    key_rows = projected[:, :, head_width : 2 * head_width]
    value_rows = projected[:, :, 2 * head_width :]
    offset = lax.axis_index("expert") * row_cells
    own_positions = offset + jnp.arange(row_cells, dtype=jnp.int32)
    start_state = (
        jnp.full((tables, head_count, row_cells), -1e30, jnp.float32),
        jnp.zeros((tables, head_count, row_cells), jnp.float32),
        jnp.zeros((tables, head_count, row_cells, DH), jnp.float32),
    )
    key_piece = lax.all_gather(key_rows, "expert", axis=0, tiled=True)
    value_piece = lax.all_gather(value_rows, "expert", axis=0, tiled=True)
    piece_len = key_piece.shape[0]
    block_len = math.gcd(piece_len, 512)
    block_count = piece_len // block_len
    key_blocks = key_piece.reshape(block_count, block_len, tables, head_count, DH)
    value_blocks = value_piece.reshape(block_count, block_len, tables, head_count, DH)
    block_starts = jnp.arange(block_count, dtype=jnp.int32) * block_len

    def step(carried, block_item):
        running_max, running_sum, accum = carried
        key_block, value_block, block_first = block_item
        scores = (
            jnp.einsum("qshd,kshd->shqk", queries, key_block, preferred_element_type=jnp.float32)
            * score_scale
        )
        key_valid = (block_first + jnp.arange(block_len, dtype=jnp.int32))[None, :] < lengths[
            :, None
        ]
        scores = jnp.where(key_valid[:, None, None, :], scores, -jnp.inf)
        new_max = jnp.maximum(running_max, jnp.max(scores, axis=-1))
        factor = jnp.exp(running_max - new_max)
        exp_scores = jnp.exp(scores - new_max[..., None])
        running_sum = running_sum * factor + jnp.sum(exp_scores, axis=-1)
        accum = accum * factor[..., None] + jnp.einsum(
            "shqk,kshd->shqd",
            exp_scores.astype(jnp.bfloat16),
            value_block,
            preferred_element_type=jnp.float32,
        )
        return ((new_max, running_sum, accum), None)

    finished, _ = lax.scan(step, start_state, (key_blocks, value_blocks, block_starts))
    running_max, running_sum, accum = finished
    normalized = accum / running_sum[..., None]
    live = own_positions[None, :] < lengths[:, None]
    normalized = jnp.where(live[:, None, :, None], normalized, 0.0)
    attended = (
        jnp.transpose(normalized, (2, 0, 1, 3))
        .reshape(row_cells, tables, head_width)
        .astype(jnp.bfloat16)
    )
    count_rows = cell_count * lax.axis_size("head")
    product = jnp.dot(
        attended.reshape(count_rows * tables, head_width), w_out, preferred_element_type=jnp.float32
    )
    summed = lax.psum_scatter(
        product.reshape(count_rows, tables, model_width).astype(jnp.bfloat16),
        "head",
        scatter_dimension=0,
        tiled=True,
    ).astype(jnp.float32)
    residual = table_cells.astype(jnp.float32) + summed
    mean_square = jnp.mean(residual * residual, axis=-1, keepdims=True)
    normed = (residual * lax.rsqrt(mean_square + 1e-06) * norm_gain.astype(jnp.float32)).astype(
        jnp.bfloat16
    )
    rows_dev = cell_count * tables
    normed_rows = normed.reshape(rows_dev, model_width)
    expert_count = lax.axis_size("expert") * lax.axis_size("head") // 2
    slot_cap = 2 * max(1, rows_dev // expert_count)
    target = expert_of_cell.reshape(rows_dev) * slot_cap + slot_of_cell.reshape(rows_dev)
    slot_table = (
        jnp.arange(expert_count * slot_cap, dtype=jnp.int32)[:, None] == target[None, :]
    ).astype(jnp.bfloat16)
    send_rows = jnp.dot(slot_table, normed_rows, preferred_element_type=jnp.float32).astype(
        jnp.bfloat16
    )
    gate_half = w_gate[0]
    up_half = w_up[0]
    down_half = w_down[0]
    split_rows = send_rows.reshape(2 * expert_count, slot_cap // 2, model_width)
    received = lax.all_to_all(
        split_rows, ("expert", "head"), split_axis=0, concat_axis=0, tiled=True
    )
    item_count = received.shape[1]
    partner_rows = from_partner(received, "head", 0)
    apply_received = jnp.concatenate([received, partner_rows], axis=1)
    sources = apply_received.shape[0]
    apply_item_count = apply_received.shape[1]
    flat_rows = apply_received.reshape(sources * apply_item_count, model_width)
    computed = expert_half(flat_rows, gate_half, up_half, down_half).reshape(
        sources, apply_item_count, model_width
    )
    returned = from_partner(computed[:, item_count:], "head", 0)
    merged = (computed[:, :item_count].astype(jnp.float32) + returned.astype(jnp.float32)).astype(
        jnp.bfloat16
    )
    gathered = lax.all_to_all(merged, ("expert", "head"), split_axis=0, concat_axis=0, tiled=True)
    combined = gathered.reshape(expert_count * slot_cap, model_width)
    expert_out = lax.dot_general(
        slot_table, combined, (((0,), (0,)), ((), ())), preferred_element_type=jnp.float32
    )
    updated = (residual.reshape(rows_dev, model_width) + expert_out).astype(jnp.bfloat16)
    return updated.reshape(cell_count, tables, model_width)


def solution(mesh):
    placed = (
        P(("expert", "head"), None, None),
        P(None, "head"),
        P(None, "head"),
        P(None, "head"),
        P("head", None),
        P(),
        P(("expert", "head"), None, None),
        P(("expert", "head"), None, None),
        P(("expert", "head"), None, None),
        P(),
        P(("expert", "head"), None),
        P(("expert", "head"), None),
    )
    pairs = mesh.shape["expert"] == 4 and mesh.shape["head"] == 8
    return jax.shard_map(
        paired_shards if pairs else shards,
        mesh=mesh,
        in_specs=placed,
        out_specs=P(("expert", "head"), None, None),
        check_vma=False,
    )
```

```python
import functools
import math

import jax
import jax.numpy as jnp
from jax import lax
from jax.experimental import pallas as pl
from jax.experimental.pallas import tpu as pltpu
from jax.sharding import PartitionSpec as P

DH = 128
VMEM = pl.BlockSpec(memory_space=pltpu.VMEM)
SMEM = pl.BlockSpec(memory_space=pltpu.SMEM)
ROWS_BY_ROWS = (((1,), (1,)), ((), ()))


def local_call(body, outs, args, specs, flops, scratch=(), grant=60):
    moved = sum(a.size * a.dtype.itemsize for a in list(args) + list(outs))
    return pl.pallas_call(
        body,
        out_shape=outs,
        in_specs=specs,
        out_specs=[VMEM] * len(outs),
        scratch_shapes=list(scratch),
        compiler_params=pltpu.CompilerParams(vmem_limit_bytes=grant * 1024 * 1024),
        cost_estimate=pl.CostEstimate(flops=flops, bytes_accessed=moved, transcendentals=0),
    )(*args)


def shape_of(dims, dtype=jnp.bfloat16):
    return jax.ShapeDtypeStruct(dims, dtype)


def swap_cores(block):
    count = lax.axis_size("head")
    return lax.ppermute(block, "head", [(h, h ^ 1) for h in range(count)])


def neighbours(block, first):
    planes = lax.axis_size("head") // 2
    route = []
    for low in range(first, planes - 1, 2):
        for core in range(2):
            here, there = 2 * low + core, 2 * low + 2 + core
            route += [(here, there), (there, here)]
    return lax.ppermute(block, "head", route)


def outwards(block):
    route = [(2 * a + core, 2 * b + core) for a, b in ((1, 0), (2, 3)) for core in range(2)]
    return lax.ppermute(block, "head", route)


def across_z(block, bits):
    count = lax.axis_size("head")
    return lax.ppermute(block, "head", [(h, h ^ (2 * bits)) for h in range(count)])


def in_plane(block, bits):
    count = lax.axis_size("expert")
    return lax.ppermute(block, "expert", [(e, e ^ bits) for e in range(count)])


def stack_body(*refs):
    half = refs[0].shape[0] // 2
    for index, ref in enumerate(refs[:-2]):
        for side in range(2):
            refs[side - 2][pl.ds(index * half, half), :] = ref[pl.ds(side * half, half), :]


def stack(blocks):
    rows, width = blocks[0].shape
    shape = shape_of((len(blocks) * rows // 2, width))
    return local_call(stack_body, [shape] * 2, blocks, [VMEM] * len(blocks), 0)


def choose_body(place_ref, *refs):
    out_ref = refs[-1]
    for side in range(2):
        start = pl.multiple_of((place_ref[0] ^ side) * DH, DH)
        for index, ref in enumerate(refs[:-1]):
            out_ref[:, pl.ds((3 * side + index) * DH, DH)] = ref[:, pl.ds(start, DH)]


def project_body(pieces, half, *refs):
    inputs, weight_ref, outs = refs[: 2 * pieces], refs[2 * pieces], refs[2 * pieces + 1 :]
    width = weight_ref.shape[1] // 2
    rows = []
    for table in range(2):
        for piece in range(pieces):
            for side in range(2):
                rows.append(inputs[2 * piece + side][pl.ds(table * half, half), :])
    mixed = jnp.dot(
        jnp.concatenate(rows, axis=0), weight_ref[...], preferred_element_type=jnp.float32
    ).astype(jnp.bfloat16)
    count = pieces * 2 * half
    for table in range(2):
        for side in range(2):
            outs[2 * table + side][...] = mixed[
                table * count : (table + 1) * count, side * width : (side + 1) * width
            ]


def project(blocks, weight):
    pieces, half, width = len(blocks), blocks[0][0].shape[0] // 2, weight.shape[1] // 2
    args = [block for pair in blocks for block in pair] + [weight]
    return local_call(
        functools.partial(project_body, pieces, half),
        [shape_of((pieces * 2 * half, width))] * 4,
        args,
        [VMEM] * len(args),
        2 * pieces * 4 * half * weight.size,
        grant=20,
    )


def attend_body(block, place_ref, bias_ref, *refs):
    early, late = refs[:4], refs[4:8]
    out_ref, (keys, values) = refs[8], refs[9:]
    spot, place, core = place_ref[0], place_ref[1], place_ref[2]
    planes = 4
    half = block // 2
    for source in range(4):
        for slot in range(planes):
            span = pl.ds((slot * 4 + source) * block, block)
            rows = pl.ds(slot % 2 * block, block)
            part = (early, late)[slot // 2][source]
            keys[span, :] = part[rows, pl.ds(DH, DH)]
            values[span, :] = part[rows, pl.ds(2 * DH, DH)]
    scale = 1.0 / math.sqrt(DH) * math.log2(math.e)
    third = jnp.where(place < 2, 2, 1)
    fourth = jnp.where(place < 2, 3, 0)

    def queries(slot, source):
        rows = pl.ds(slot % 2 * block, block)
        return (early, late)[slot // 2][source][rows, pl.ds(0, DH)]

    for slot, plane in enumerate((place, place ^ 1, third, fourth)):
        for first in (0, 2):
            rows = jnp.concatenate([queries(slot, first), queries(slot, first + 1)], axis=0)
            scores = lax.dot_general(
                rows, keys[...], ROWS_BY_ROWS, preferred_element_type=jnp.float32
            )
            scores = scores + bias_ref[...]
            top = jnp.max(scores, axis=1, keepdims=True)
            weights = jnp.exp2((scores - top) * scale)
            total = jnp.sum(weights, axis=1, keepdims=True)
            mixed = jnp.dot(
                weights.astype(jnp.bfloat16), values[...], preferred_element_type=jnp.float32
            )
            mixed = (mixed / total).astype(jnp.bfloat16)
            for index in range(4):
                source, side = first + index // 2, index % 2
                device = (spot ^ source) * 2 * planes + 2 * plane + (core ^ side)
                start = pl.multiple_of(device * half, half)
                out_ref[pl.ds(start, half), :] = mixed[index * half : (index + 1) * half]


def join_body(planes, place_ref, own_ref, live_ref, target_ref, gain_ref, heads_ref, *refs):
    weights = (refs[:9], refs[9:18])
    residual_ref, send_ref, joined = refs[18:]
    spot, place, core = place_ref[0], place_ref[1], place_ref[2]
    mine = spot // 2
    block, quarter = joined.shape[0] // 2, weights[0][1].shape[1]
    pair = 2 * DH
    for source in range(4):
        rows = pl.ds(pl.multiple_of((source // 2 ^ mine) * block, block), block)
        for head in range(2 * planes):
            columns = pl.ds(head * pair + source % 2 * DH, DH)
            joined[rows, columns] = heads_ref[
                pl.ds((source * 2 * planes + head) * block, block), :
            ]
    joined[...] = jnp.where(live_ref[...] > 0, joined[...].astype(jnp.float32), 0.0).astype(
        jnp.bfloat16
    )
    squares = jnp.zeros((2 * block, 1), jnp.float32)
    for bits in range(4):
        columns = pl.ds(pl.multiple_of((spot ^ bits) * quarter, quarter), quarter)
        total = own_ref[:, columns].astype(jnp.float32)
        for side in range(2):
            for offset in range(planes):
                device = 2 * (place ^ offset) + (core ^ side)
                start = pl.multiple_of(device * pair, pair)
                if offset == 0:
                    total += jnp.dot(
                        joined[:, pl.ds(start, pair)],
                        weights[side][0][:, columns],
                        preferred_element_type=jnp.float32,
                    )
                    continue
                for half in range(2):
                    total += jnp.dot(
                        joined[:, pl.ds(start + half * DH, DH)],
                        weights[side][1 + 2 * bits + half][pl.ds((offset - 1) * DH, DH), :],
                        preferred_element_type=jnp.float32,
                    )
        residual_ref[:, columns] = total
        squares += jnp.sum(total * total, axis=1, keepdims=True)
    residual = residual_ref[...]
    mean_square = squares / residual.shape[1]
    normed = residual * lax.rsqrt(mean_square + 1e-06) * gain_ref[...].astype(jnp.float32)
    slots = send_ref.shape[0]
    chosen = lax.broadcasted_iota(jnp.int32, (slots, 2 * block), 0) == target_ref[...]
    send_ref[...] = jnp.dot(
        chosen.astype(jnp.float32).astype(jnp.bfloat16),
        normed.astype(jnp.bfloat16),
        preferred_element_type=jnp.float32,
    ).astype(jnp.bfloat16)


def expert_body(rows_ref, *refs):
    sources, out_ref, held, arrivals = refs[:6], refs[6], refs[7:13], refs[13]
    copies = [
        pltpu.make_async_copy(source, place, arrivals.at[index])
        for index, (source, place) in enumerate(zip(sources, held))
    ]
    for copy in copies:
        copy.start()
    rows = rows_ref[...]
    total = jnp.zeros(rows.shape, jnp.float32)
    for half in range(2):
        gate_ref, up_ref, down_ref = held[3 * half : 3 * half + 3]
        copies[3 * half].wait()
        gate = lax.dot_general(
            rows, gate_ref[...], ROWS_BY_ROWS, preferred_element_type=jnp.float32
        )
        copies[3 * half + 1].wait()
        up = lax.dot_general(rows, up_ref[...], ROWS_BY_ROWS, preferred_element_type=jnp.float32)
        hidden = (gate / (1.0 + jnp.exp(-gate)) * up).astype(jnp.bfloat16)
        copies[3 * half + 2].wait()
        total += jnp.dot(hidden, down_ref[...], preferred_element_type=jnp.float32)
    out_ref[...] = total.astype(jnp.bfloat16)


def finish_body(residual_ref, target_ref, blocks_ref, place_ref, out_ref):
    slots, rows = blocks_ref.shape[0], residual_ref.shape[0]
    chosen = target_ref[...] == lax.broadcasted_iota(jnp.int32, (rows, slots), 1)
    expert_out = jnp.dot(
        chosen.astype(jnp.float32).astype(jnp.bfloat16),
        blocks_ref[...],
        preferred_element_type=jnp.float32,
    )
    updated = residual_ref[...] + expert_out
    mine, other = updated[: rows // 2], updated[rows // 2 :]
    in_order = place_ref[0] < 2
    out_ref[:, 0, :] = jnp.where(in_order, mine, other).astype(jnp.bfloat16)
    out_ref[:, 1, :] = jnp.where(in_order, other, mine).astype(jnp.bfloat16)


def paired_shards(
    table_cells,
    w_query,
    w_key,
    w_value,
    w_out,
    norm_gain,
    w_gate,
    w_up,
    w_down,
    lengths,
    expert_of_cell,
    slot_of_cell,
):
    cells, tables, width = table_cells.shape
    heads = lax.axis_size("head")
    planes = heads // 2
    spot, place_head = lax.axis_index("expert"), lax.axis_index("head")
    mine, parity = spot // 2, spot % 2
    place, core = place_head // 2, place_head % 2

    rows_dev = cells * tables
    first, second = table_cells[:, 0], table_cells[:, 1]
    own = jnp.where(
        mine == 0,
        jnp.concatenate([first, second], axis=0),
        jnp.concatenate([second, first], axis=0),
    )

    weight = pl.pallas_call(
        choose_body,
        out_shape=pltpu.VMEM((width, 6 * DH), w_query.dtype),
        in_specs=[SMEM] + [VMEM] * 3,
        out_specs=VMEM,
        compiler_params=pltpu.CompilerParams(vmem_limit_bytes=56 * 1024 * 1024),
        cost_estimate=pl.CostEstimate(
            flops=0, bytes_accessed=24 * w_query.size, transcendentals=0
        ),
    )(parity.reshape(1).astype(jnp.int32), w_query, w_key, w_value)

    def spread(outs):
        return [outs[0]] + [in_plane(outs[bits], bits) for bits in range(1, 4)]

    block = 2 * cells
    low = place < 2
    held = jnp.stack([place, place ^ 1, jnp.where(low, 2, 1), jnp.where(low, 3, 0)])
    sources = jnp.arange(4, dtype=jnp.int32)[None, :, None, None]
    sides = jnp.arange(2, dtype=jnp.int32)[None, None, :, None]
    cell = jnp.arange(cells, dtype=jnp.int32)[None, None, None, :]
    device = (spot ^ sources) * heads + 2 * held[:, None, None, None] + (core ^ sides)
    count = planes * 4 * block
    positions = (device * cells + cell).reshape(1, count)
    bias = jnp.where(positions < lengths[mine], 0.0, -jnp.inf).astype(jnp.float32)
    where = jnp.stack([spot, place, core]).astype(jnp.int32)
    own_positions = (spot * heads + place_head) * cells + jnp.arange(cells, dtype=jnp.int32)
    table_order = jnp.stack([mine, 1 - mine])
    live = (own_positions[None, :] < lengths[table_order][:, None]).astype(jnp.int32)
    expert_count = lax.axis_size("expert") * heads // 2
    slot_cap = 2 * max(1, rows_dev // expert_count)
    target = (expert_of_cell * slot_cap + slot_of_cell).T
    target = jnp.where(mine == 0, target, target[::-1]).reshape(1, rows_dev)
    slots = expert_count * slot_cap
    live, target, target_column = live.reshape(rows_dev, 1), target, target.reshape(rows_dev, 1)
    gain = norm_gain.reshape(1, width)

    inside = (place == 1) | (place == 2)
    beside = neighbours(own, 0)
    inner = neighbours(own, 1)
    beside_too = swap_cores(beside)
    quarter = width // 4
    part = lax.dynamic_slice_in_dim(w_out, spot * quarter, quarter, 1)
    parts = [across_z(part, bits) for bits in range(1, planes)]
    small = (bias, where, live, target, target_column, gain)
    halves = [w_gate[0], w_up[0], w_down[0]]
    others = [swap_cores(w) for w in halves]
    inner, small, weight, others[0], parts[0] = lax.optimization_barrier(
        (inner, small, weight, others[0], parts[0])
    )
    bias, where, live, target, target_column, gain = small
    outer = outwards(inner)
    inner_far = neighbours(beside, 1)
    early_out = project([(own, swap_cores(own)), (beside, beside_too)], weight)
    early = spread(early_out)
    outer_far = outwards(inner_far)
    third = jnp.where(inside, inner, outer)
    third_too = swap_cores(third)
    outer_far, third_too, others[1] = lax.optimization_barrier(
        (outer_far, third_too, others[1])
    )
    fourth = jnp.where(inside, inner_far, outer_far)
    late_out = project([(third, third_too), (fourth, swap_cores(fourth))], weight)
    late_out, early, parts[1] = lax.optimization_barrier((late_out, early, parts[1]))
    late = spread(late_out)

    parts, late, others[2] = lax.optimization_barrier((parts, late, others[2]))
    expert_weights = halves + others
    far = stack(parts)
    far, late = lax.optimization_barrier((far, late))
    shared = early + late
    fars = [[in_plane(half, bits) for half in far] for bits in (1, 2)]
    everyone = ("expert", "head")
    attended = local_call(
        functools.partial(attend_body, block),
        [shape_of((count, DH))],
        [where, bias] + shared,
        [SMEM] + [VMEM] * 9,
        4 * count * count * DH,
        [pltpu.VMEM((count, DH), jnp.bfloat16)] * 2,
        grant=60,
    )[0]
    fars, _ = lax.optimization_barrier((fars, attended))
    across = [in_plane(fars[1][0], 1), in_plane(fars[0][1], 2)]
    same = [w_out, *far, *fars[0], *fars[1], *across]
    out_weights = same + [swap_cores(w) for w in same]
    arrived = lax.all_to_all(attended, everyone, 0, 0, tiled=True)

    residual, send_rows = local_call(
        functools.partial(join_body, planes),
        [shape_of((rows_dev, width), jnp.float32), shape_of((slots, width))],
        [
            where,
            own,
            live,
            target,
            gain,
            arrived,
        ]
        + out_weights,
        [SMEM] + [VMEM] * 23,
        2 * rows_dev * width * (width + slots),
        [pltpu.VMEM((rows_dev, width), jnp.bfloat16)],
    )

    received = lax.all_to_all(send_rows, everyone, 0, 0, tiled=True)
    computed = local_call(
        expert_body,
        [shape_of((slots, width))],
        [received] + expert_weights,
        [VMEM] + [pl.BlockSpec(memory_space=pl.ANY)] * 6,
        2 * slots * 6 * w_gate.size,
        [pltpu.VMEM(w.shape, w.dtype) for w in expert_weights] + [pltpu.SemaphoreType.DMA((6,))],
        grant=60,
    )[0]
    gathered = lax.all_to_all(computed, everyone, 0, 0, tiled=True)
    return local_call(
        finish_body,
        [shape_of((cells, tables, width))],
        [residual, target_column, gathered, where],
        [VMEM] * 3 + [SMEM],
        2 * rows_dev * width * slots,
        grant=48,
    )[0]


def from_partner(block, axis, bit):
    count = lax.axis_size(axis)
    route = []
    for low in range(count):
        high = low | 1 << bit
        if high != low and high < count:
            route += [(low, high), (high, low)]
    return lax.ppermute(block, axis, route)


def expert_half(slot_rows, gate_half, up_half, down_half):
    contract_rows = (((1,), (1,)), ((), ()))
    gate_t = lax.dot_general(
        gate_half, slot_rows, contract_rows, preferred_element_type=jnp.float32
    )
    up_t = lax.dot_general(up_half, slot_rows, contract_rows, preferred_element_type=jnp.float32)
    hidden = (jax.nn.silu(gate_t) * up_t).astype(jnp.bfloat16)
    product = lax.dot_general(
        hidden, down_half, (((0,), (0,)), ((), ())), preferred_element_type=jnp.float32
    )
    return product.astype(jnp.bfloat16)


def shards(
    table_cells,
    w_query,
    w_key,
    w_value,
    w_out,
    norm_gain,
    w_gate,
    w_up,
    w_down,
    lengths,
    expert_of_cell,
    slot_of_cell,
):
    cell_count, tables, model_width = table_cells.shape
    head_width = w_query.shape[1]
    head_count = head_width // DH
    score_scale = 1.0 / math.sqrt(DH)
    joined = jnp.concatenate([w_query, w_key, w_value], axis=1)
    shard_rows = lax.all_gather(table_cells, "head", axis=0, tiled=True)
    rows_here = shard_rows.shape[0]
    mixed_rows = jnp.dot(
        shard_rows.reshape(rows_here * tables, model_width),
        joined,
        preferred_element_type=jnp.float32,
    )
    projected = mixed_rows.astype(jnp.bfloat16).reshape(rows_here, tables, 3 * head_width)
    row_cells = projected.shape[0]
    queries = projected[:, :, :head_width].reshape(row_cells, tables, head_count, DH)
    key_rows = projected[:, :, head_width : 2 * head_width]
    value_rows = projected[:, :, 2 * head_width :]
    offset = lax.axis_index("expert") * row_cells
    own_positions = offset + jnp.arange(row_cells, dtype=jnp.int32)
    start_state = (
        jnp.full((tables, head_count, row_cells), -1e30, jnp.float32),
        jnp.zeros((tables, head_count, row_cells), jnp.float32),
        jnp.zeros((tables, head_count, row_cells, DH), jnp.float32),
    )
    key_piece = lax.all_gather(key_rows, "expert", axis=0, tiled=True)
    value_piece = lax.all_gather(value_rows, "expert", axis=0, tiled=True)
    piece_len = key_piece.shape[0]
    block_len = math.gcd(piece_len, 512)
    block_count = piece_len // block_len
    key_blocks = key_piece.reshape(block_count, block_len, tables, head_count, DH)
    value_blocks = value_piece.reshape(block_count, block_len, tables, head_count, DH)
    block_starts = jnp.arange(block_count, dtype=jnp.int32) * block_len

    def step(carried, block_item):
        running_max, running_sum, accum = carried
        key_block, value_block, block_first = block_item
        scores = (
            jnp.einsum("qshd,kshd->shqk", queries, key_block, preferred_element_type=jnp.float32)
            * score_scale
        )
        key_valid = (block_first + jnp.arange(block_len, dtype=jnp.int32))[None, :] < lengths[
            :, None
        ]
        scores = jnp.where(key_valid[:, None, None, :], scores, -jnp.inf)
        new_max = jnp.maximum(running_max, jnp.max(scores, axis=-1))
        factor = jnp.exp(running_max - new_max)
        exp_scores = jnp.exp(scores - new_max[..., None])
        running_sum = running_sum * factor + jnp.sum(exp_scores, axis=-1)
        accum = accum * factor[..., None] + jnp.einsum(
            "shqk,kshd->shqd",
            exp_scores.astype(jnp.bfloat16),
            value_block,
            preferred_element_type=jnp.float32,
        )
        return ((new_max, running_sum, accum), None)

    finished, _ = lax.scan(step, start_state, (key_blocks, value_blocks, block_starts))
    running_max, running_sum, accum = finished
    normalized = accum / running_sum[..., None]
    live = own_positions[None, :] < lengths[:, None]
    normalized = jnp.where(live[:, None, :, None], normalized, 0.0)
    attended = (
        jnp.transpose(normalized, (2, 0, 1, 3))
        .reshape(row_cells, tables, head_width)
        .astype(jnp.bfloat16)
    )
    count_rows = cell_count * lax.axis_size("head")
    product = jnp.dot(
        attended.reshape(count_rows * tables, head_width), w_out, preferred_element_type=jnp.float32
    )
    summed = lax.psum_scatter(
        product.reshape(count_rows, tables, model_width).astype(jnp.bfloat16),
        "head",
        scatter_dimension=0,
        tiled=True,
    ).astype(jnp.float32)
    residual = table_cells.astype(jnp.float32) + summed
    mean_square = jnp.mean(residual * residual, axis=-1, keepdims=True)
    normed = (residual * lax.rsqrt(mean_square + 1e-06) * norm_gain.astype(jnp.float32)).astype(
        jnp.bfloat16
    )
    rows_dev = cell_count * tables
    normed_rows = normed.reshape(rows_dev, model_width)
    expert_count = lax.axis_size("expert") * lax.axis_size("head") // 2
    slot_cap = 2 * max(1, rows_dev // expert_count)
    target = expert_of_cell.reshape(rows_dev) * slot_cap + slot_of_cell.reshape(rows_dev)
    slot_table = (
        jnp.arange(expert_count * slot_cap, dtype=jnp.int32)[:, None] == target[None, :]
    ).astype(jnp.bfloat16)
    send_rows = jnp.dot(slot_table, normed_rows, preferred_element_type=jnp.float32).astype(
        jnp.bfloat16
    )
    gate_half = w_gate[0]
    up_half = w_up[0]
    down_half = w_down[0]
    split_rows = send_rows.reshape(2 * expert_count, slot_cap // 2, model_width)
    received = lax.all_to_all(
        split_rows, ("expert", "head"), split_axis=0, concat_axis=0, tiled=True
    )
    item_count = received.shape[1]
    partner_rows = from_partner(received, "head", 0)
    apply_received = jnp.concatenate([received, partner_rows], axis=1)
    sources = apply_received.shape[0]
    apply_item_count = apply_received.shape[1]
    flat_rows = apply_received.reshape(sources * apply_item_count, model_width)
    computed = expert_half(flat_rows, gate_half, up_half, down_half).reshape(
        sources, apply_item_count, model_width
    )
    returned = from_partner(computed[:, item_count:], "head", 0)
    merged = (computed[:, :item_count].astype(jnp.float32) + returned.astype(jnp.float32)).astype(
        jnp.bfloat16
    )
    gathered = lax.all_to_all(merged, ("expert", "head"), split_axis=0, concat_axis=0, tiled=True)
    combined = gathered.reshape(expert_count * slot_cap, model_width)
    expert_out = lax.dot_general(
        slot_table, combined, (((0,), (0,)), ((), ())), preferred_element_type=jnp.float32
    )
    updated = (residual.reshape(rows_dev, model_width) + expert_out).astype(jnp.bfloat16)
    return updated.reshape(cell_count, tables, model_width)


def solution(mesh):
    placed = (
        P(("expert", "head"), None, None),
        P(None, "head"),
        P(None, "head"),
        P(None, "head"),
        P("head", None),
        P(),
        P(("expert", "head"), None, None),
        P(("expert", "head"), None, None),
        P(("expert", "head"), None, None),
        P(),
        P(("expert", "head"), None),
        P(("expert", "head"), None),
    )
    pairs = mesh.shape["expert"] == 4 and mesh.shape["head"] == 8
    return jax.shard_map(
        paired_shards if pairs else shards,
        mesh=mesh,
        in_specs=placed,
        out_specs=P(("expert", "head"), None, None),
        check_vma=False,
    )
```

```python
import functools
import math

import jax
import jax.numpy as jnp
from jax import lax
from jax.experimental import pallas as pl
from jax.experimental.pallas import tpu as pltpu
from jax.sharding import PartitionSpec as P

DH = 128
VMEM = pl.BlockSpec(memory_space=pltpu.VMEM)
SMEM = pl.BlockSpec(memory_space=pltpu.SMEM)
ROWS_BY_ROWS = (((1,), (1,)), ((), ()))


def local_call(body, outs, args, specs, flops, scratch=(), grant=60):
    moved = sum(a.size * a.dtype.itemsize for a in list(args) + list(outs))
    return pl.pallas_call(
        body,
        out_shape=outs,
        in_specs=specs,
        out_specs=[VMEM] * len(outs),
        scratch_shapes=list(scratch),
        compiler_params=pltpu.CompilerParams(vmem_limit_bytes=grant * 1024 * 1024),
        cost_estimate=pl.CostEstimate(flops=flops, bytes_accessed=moved, transcendentals=0),
    )(*args)


def shape_of(dims, dtype=jnp.bfloat16):
    return jax.ShapeDtypeStruct(dims, dtype)


def swap_cores(block):
    count = lax.axis_size("head")
    return lax.ppermute(block, "head", [(h, h ^ 1) for h in range(count)])


def neighbours(block, first):
    planes = lax.axis_size("head") // 2
    route = []
    for low in range(first, planes - 1, 2):
        for core in range(2):
            here, there = 2 * low + core, 2 * low + 2 + core
            route += [(here, there), (there, here)]
    return lax.ppermute(block, "head", route)


def outwards(block):
    route = [(2 * a + core, 2 * b + core) for a, b in ((1, 0), (2, 3)) for core in range(2)]
    return lax.ppermute(block, "head", route)


def across_z(block, bits):
    count = lax.axis_size("head")
    return lax.ppermute(block, "head", [(h, h ^ (2 * bits)) for h in range(count)])


def in_plane(block, bits):
    count = lax.axis_size("expert")
    return lax.ppermute(block, "expert", [(e, e ^ bits) for e in range(count)])


def stack_body(*refs):
    half = refs[0].shape[0] // 2
    for index, ref in enumerate(refs[:-2]):
        for side in range(2):
            refs[side - 2][pl.ds(index * half, half), :] = ref[pl.ds(side * half, half), :]


def stack(blocks):
    rows, width = blocks[0].shape
    shape = shape_of((len(blocks) * rows // 2, width))
    return local_call(stack_body, [shape] * 2, blocks, [VMEM] * len(blocks), 0)


def choose_body(place_ref, *refs):
    out_ref = refs[-1]
    for side in range(2):
        start = pl.multiple_of((place_ref[0] ^ side) * DH, DH)
        for index, ref in enumerate(refs[:-1]):
            out_ref[:, pl.ds((3 * side + index) * DH, DH)] = ref[:, pl.ds(start, DH)]


def project_body(pieces, half, *refs):
    inputs, weight_ref, outs = refs[: 2 * pieces], refs[2 * pieces], refs[2 * pieces + 1 :]
    width = weight_ref.shape[1] // 2
    rows = []
    for table in range(2):
        for piece in range(pieces):
            for side in range(2):
                rows.append(inputs[2 * piece + side][pl.ds(table * half, half), :])
    mixed = jnp.dot(
        jnp.concatenate(rows, axis=0), weight_ref[...], preferred_element_type=jnp.float32
    ).astype(jnp.bfloat16)
    count = pieces * 2 * half
    for table in range(2):
        for side in range(2):
            outs[2 * table + side][...] = mixed[
                table * count : (table + 1) * count, side * width : (side + 1) * width
            ]


def project(blocks, weight):
    pieces, half, width = len(blocks), blocks[0][0].shape[0] // 2, weight.shape[1] // 2
    args = [block for pair in blocks for block in pair] + [weight]
    return local_call(
        functools.partial(project_body, pieces, half),
        [shape_of((pieces * 2 * half, width))] * 4,
        args,
        [VMEM] * len(args),
        2 * pieces * 4 * half * weight.size,
        grant=20,
    )


def attend_body(block, place_ref, bias_ref, *refs):
    early, late = refs[:4], refs[4:8]
    out_ref, (keys, values) = refs[8], refs[9:]
    spot, place, core = place_ref[0], place_ref[1], place_ref[2]
    planes = 4
    half = block // 2
    for source in range(4):
        for slot in range(planes):
            span = pl.ds((slot * 4 + source) * block, block)
            rows = pl.ds(slot % 2 * block, block)
            part = (early, late)[slot // 2][source]
            keys[span, :] = part[rows, pl.ds(DH, DH)]
            values[span, :] = part[rows, pl.ds(2 * DH, DH)]
    scale = 1.0 / math.sqrt(DH) * math.log2(math.e)
    third = jnp.where(place < 2, 2, 1)
    fourth = jnp.where(place < 2, 3, 0)

    def queries(slot, source):
        rows = pl.ds(slot % 2 * block, block)
        return (early, late)[slot // 2][source][rows, pl.ds(0, DH)]

    for slot, plane in enumerate((place, place ^ 1, third, fourth)):
        for first in (0, 2):
            rows = jnp.concatenate([queries(slot, first), queries(slot, first + 1)], axis=0)
            scores = lax.dot_general(
                rows, keys[...], ROWS_BY_ROWS, preferred_element_type=jnp.float32
            )
            scores = scores + bias_ref[...]
            top = jnp.max(scores, axis=1, keepdims=True)
            weights = jnp.exp2((scores - top) * scale)
            total = jnp.sum(weights, axis=1, keepdims=True)
            mixed = jnp.dot(
                weights.astype(jnp.bfloat16), values[...], preferred_element_type=jnp.float32
            )
            mixed = (mixed / total).astype(jnp.bfloat16)
            for index in range(4):
                source, side = first + index // 2, index % 2
                device = (spot ^ source) * 2 * planes + 2 * plane + (core ^ side)
                start = pl.multiple_of(device * half, half)
                out_ref[pl.ds(start, half), :] = mixed[index * half : (index + 1) * half]


def join_body(planes, place_ref, own_ref, live_ref, target_ref, gain_ref, heads_ref, *refs):
    weights = (refs[:9], refs[9:18])
    residual_ref, send_ref, joined = refs[18:]
    spot, place, core = place_ref[0], place_ref[1], place_ref[2]
    mine = spot // 2
    block, quarter = joined.shape[0] // 2, weights[0][1].shape[1]
    pair = 2 * DH
    depth = (planes - 1) * DH
    side_width = planes * pair
    for source in range(4):
        rows = pl.ds(pl.multiple_of((source // 2 ^ mine) * block, block), block)
        half = source % 2
        for side in range(2):
            for offset in range(planes):
                device = 2 * (place ^ offset) + (core ^ side)
                start = pl.multiple_of((source * 2 * planes + device) * block, block)
                inner = half * DH if offset == 0 else pair + half * depth + (offset - 1) * DH
                joined[rows, pl.ds(side * side_width + inner, DH)] = heads_ref[
                    pl.ds(start, block), :
                ]
    joined[...] = jnp.where(live_ref[...] > 0, joined[...].astype(jnp.float32), 0.0).astype(
        jnp.bfloat16
    )
    squares = jnp.zeros((2 * block, 1), jnp.float32)
    for bits in range(4):
        columns = pl.ds(pl.multiple_of((spot ^ bits) * quarter, quarter), quarter)
        total = own_ref[:, columns].astype(jnp.float32)
        for side in range(2):
            total += jnp.dot(
                joined[:, pl.ds(side * side_width, pair)],
                weights[side][0][:, columns],
                preferred_element_type=jnp.float32,
            )
            for half in range(2):
                total += jnp.dot(
                    joined[:, pl.ds(side * side_width + pair + half * depth, depth)],
                    weights[side][1 + 2 * bits + half][...],
                    preferred_element_type=jnp.float32,
                )
        residual_ref[:, columns] = total
        squares += jnp.sum(total * total, axis=1, keepdims=True)
    residual = residual_ref[...]
    mean_square = squares / residual.shape[1]
    normed = residual * lax.rsqrt(mean_square + 1e-06) * gain_ref[...].astype(jnp.float32)
    slots = send_ref.shape[0]
    chosen = lax.broadcasted_iota(jnp.int32, (slots, 2 * block), 0) == target_ref[...]
    send_ref[...] = jnp.dot(
        chosen.astype(jnp.float32).astype(jnp.bfloat16),
        normed.astype(jnp.bfloat16),
        preferred_element_type=jnp.float32,
    ).astype(jnp.bfloat16)


def expert_body(rows_ref, *refs):
    sources, out_ref, held, arrivals = refs[:6], refs[6], refs[7:13], refs[13]
    copies = [
        pltpu.make_async_copy(source, place, arrivals.at[index])
        for index, (source, place) in enumerate(zip(sources, held))
    ]
    for copy in copies:
        copy.start()
    rows = rows_ref[...]
    total = jnp.zeros(rows.shape, jnp.float32)
    for half in range(2):
        gate_ref, up_ref, down_ref = held[3 * half : 3 * half + 3]
        copies[3 * half].wait()
        gate = lax.dot_general(
            rows, gate_ref[...], ROWS_BY_ROWS, preferred_element_type=jnp.float32
        )
        copies[3 * half + 1].wait()
        up = lax.dot_general(rows, up_ref[...], ROWS_BY_ROWS, preferred_element_type=jnp.float32)
        hidden = (gate / (1.0 + jnp.exp(-gate)) * up).astype(jnp.bfloat16)
        copies[3 * half + 2].wait()
        total += jnp.dot(hidden, down_ref[...], preferred_element_type=jnp.float32)
    out_ref[...] = total.astype(jnp.bfloat16)


def finish_body(residual_ref, target_ref, blocks_ref, place_ref, out_ref):
    slots, rows = blocks_ref.shape[0], residual_ref.shape[0]
    chosen = target_ref[...] == lax.broadcasted_iota(jnp.int32, (rows, slots), 1)
    expert_out = jnp.dot(
        chosen.astype(jnp.float32).astype(jnp.bfloat16),
        blocks_ref[...],
        preferred_element_type=jnp.float32,
    )
    updated = residual_ref[...] + expert_out
    mine, other = updated[: rows // 2], updated[rows // 2 :]
    in_order = place_ref[0] < 2
    out_ref[:, 0, :] = jnp.where(in_order, mine, other).astype(jnp.bfloat16)
    out_ref[:, 1, :] = jnp.where(in_order, other, mine).astype(jnp.bfloat16)


def paired_shards(
    table_cells,
    w_query,
    w_key,
    w_value,
    w_out,
    norm_gain,
    w_gate,
    w_up,
    w_down,
    lengths,
    expert_of_cell,
    slot_of_cell,
):
    cells, tables, width = table_cells.shape
    heads = lax.axis_size("head")
    planes = heads // 2
    spot, place_head = lax.axis_index("expert"), lax.axis_index("head")
    mine, parity = spot // 2, spot % 2
    place, core = place_head // 2, place_head % 2

    rows_dev = cells * tables
    first, second = table_cells[:, 0], table_cells[:, 1]
    own = jnp.where(
        mine == 0,
        jnp.concatenate([first, second], axis=0),
        jnp.concatenate([second, first], axis=0),
    )

    weight = pl.pallas_call(
        choose_body,
        out_shape=pltpu.VMEM((width, 6 * DH), w_query.dtype),
        in_specs=[SMEM] + [VMEM] * 3,
        out_specs=VMEM,
        compiler_params=pltpu.CompilerParams(vmem_limit_bytes=56 * 1024 * 1024),
        cost_estimate=pl.CostEstimate(
            flops=0, bytes_accessed=24 * w_query.size, transcendentals=0
        ),
    )(parity.reshape(1).astype(jnp.int32), w_query, w_key, w_value)

    def spread(outs):
        return [outs[0]] + [in_plane(outs[bits], bits) for bits in range(1, 4)]

    block = 2 * cells
    low = place < 2
    held = jnp.stack([place, place ^ 1, jnp.where(low, 2, 1), jnp.where(low, 3, 0)])
    sources = jnp.arange(4, dtype=jnp.int32)[None, :, None, None]
    sides = jnp.arange(2, dtype=jnp.int32)[None, None, :, None]
    cell = jnp.arange(cells, dtype=jnp.int32)[None, None, None, :]
    device = (spot ^ sources) * heads + 2 * held[:, None, None, None] + (core ^ sides)
    count = planes * 4 * block
    positions = (device * cells + cell).reshape(1, count)
    bias = jnp.where(positions < lengths[mine], 0.0, -jnp.inf).astype(jnp.float32)
    where = jnp.stack([spot, place, core]).astype(jnp.int32)
    own_positions = (spot * heads + place_head) * cells + jnp.arange(cells, dtype=jnp.int32)
    table_order = jnp.stack([mine, 1 - mine])
    live = (own_positions[None, :] < lengths[table_order][:, None]).astype(jnp.int32)
    expert_count = lax.axis_size("expert") * heads // 2
    slot_cap = 2 * max(1, rows_dev // expert_count)
    target = (expert_of_cell * slot_cap + slot_of_cell).T
    target = jnp.where(mine == 0, target, target[::-1]).reshape(1, rows_dev)
    slots = expert_count * slot_cap
    live, target, target_column = live.reshape(rows_dev, 1), target, target.reshape(rows_dev, 1)
    gain = norm_gain.reshape(1, width)

    inside = (place == 1) | (place == 2)
    beside = neighbours(own, 0)
    inner = neighbours(own, 1)
    beside_too = swap_cores(beside)
    quarter = width // 4
    part = lax.dynamic_slice_in_dim(w_out, spot * quarter, quarter, 1)
    parts = [across_z(part, bits) for bits in range(1, planes)]
    small = (bias, where, live, target, target_column, gain)
    halves = [w_gate[0], w_up[0], w_down[0]]
    others = [swap_cores(w) for w in halves]
    inner, small, weight, others[0], parts[0] = lax.optimization_barrier(
        (inner, small, weight, others[0], parts[0])
    )
    bias, where, live, target, target_column, gain = small
    outer = outwards(inner)
    inner_far = neighbours(beside, 1)
    early_out = project([(own, swap_cores(own)), (beside, beside_too)], weight)
    early = spread(early_out)
    outer_far = outwards(inner_far)
    third = jnp.where(inside, inner, outer)
    third_too = swap_cores(third)
    outer_far, third_too, others[1] = lax.optimization_barrier(
        (outer_far, third_too, others[1])
    )
    fourth = jnp.where(inside, inner_far, outer_far)
    late_out = project([(third, third_too), (fourth, swap_cores(fourth))], weight)
    late_out, early, parts[1] = lax.optimization_barrier((late_out, early, parts[1]))
    late = spread(late_out)

    parts, late, others[2] = lax.optimization_barrier((parts, late, others[2]))
    expert_weights = halves + others
    far = stack(parts)
    far, late = lax.optimization_barrier((far, late))
    shared = early + late
    fars = [[in_plane(half, bits) for half in far] for bits in (1, 2)]
    everyone = ("expert", "head")
    attended = local_call(
        functools.partial(attend_body, block),
        [shape_of((count, DH))],
        [where, bias] + shared,
        [SMEM] + [VMEM] * 9,
        4 * count * count * DH,
        [pltpu.VMEM((count, DH), jnp.bfloat16)] * 2,
        grant=60,
    )[0]
    fars, _ = lax.optimization_barrier((fars, attended))
    across = [in_plane(fars[1][0], 1), in_plane(fars[0][1], 2)]
    same = [w_out, *far, *fars[0], *fars[1], *across]
    out_weights = same + [swap_cores(w) for w in same]
    arrived = lax.all_to_all(attended, everyone, 0, 0, tiled=True)

    residual, send_rows = local_call(
        functools.partial(join_body, planes),
        [shape_of((rows_dev, width), jnp.float32), shape_of((slots, width))],
        [
            where,
            own,
            live,
            target,
            gain,
            arrived,
        ]
        + out_weights,
        [SMEM] + [VMEM] * 23,
        2 * rows_dev * width * (width + slots),
        [pltpu.VMEM((rows_dev, width), jnp.bfloat16)],
    )

    received = lax.all_to_all(send_rows, everyone, 0, 0, tiled=True)
    computed = local_call(
        expert_body,
        [shape_of((slots, width))],
        [received] + expert_weights,
        [VMEM] + [pl.BlockSpec(memory_space=pl.ANY)] * 6,
        2 * slots * 6 * w_gate.size,
        [pltpu.VMEM(w.shape, w.dtype) for w in expert_weights] + [pltpu.SemaphoreType.DMA((6,))],
        grant=60,
    )[0]
    gathered = lax.all_to_all(computed, everyone, 0, 0, tiled=True)
    return local_call(
        finish_body,
        [shape_of((cells, tables, width))],
        [residual, target_column, gathered, where],
        [VMEM] * 3 + [SMEM],
        2 * rows_dev * width * slots,
        grant=48,
    )[0]


def from_partner(block, axis, bit):
    count = lax.axis_size(axis)
    route = []
    for low in range(count):
        high = low | 1 << bit
        if high != low and high < count:
            route += [(low, high), (high, low)]
    return lax.ppermute(block, axis, route)


def expert_half(slot_rows, gate_half, up_half, down_half):
    contract_rows = (((1,), (1,)), ((), ()))
    gate_t = lax.dot_general(
        gate_half, slot_rows, contract_rows, preferred_element_type=jnp.float32
    )
    up_t = lax.dot_general(up_half, slot_rows, contract_rows, preferred_element_type=jnp.float32)
    hidden = (jax.nn.silu(gate_t) * up_t).astype(jnp.bfloat16)
    product = lax.dot_general(
        hidden, down_half, (((0,), (0,)), ((), ())), preferred_element_type=jnp.float32
    )
    return product.astype(jnp.bfloat16)


def shards(
    table_cells,
    w_query,
    w_key,
    w_value,
    w_out,
    norm_gain,
    w_gate,
    w_up,
    w_down,
    lengths,
    expert_of_cell,
    slot_of_cell,
):
    cell_count, tables, model_width = table_cells.shape
    head_width = w_query.shape[1]
    head_count = head_width // DH
    score_scale = 1.0 / math.sqrt(DH)
    joined = jnp.concatenate([w_query, w_key, w_value], axis=1)
    shard_rows = lax.all_gather(table_cells, "head", axis=0, tiled=True)
    rows_here = shard_rows.shape[0]
    mixed_rows = jnp.dot(
        shard_rows.reshape(rows_here * tables, model_width),
        joined,
        preferred_element_type=jnp.float32,
    )
    projected = mixed_rows.astype(jnp.bfloat16).reshape(rows_here, tables, 3 * head_width)
    row_cells = projected.shape[0]
    queries = projected[:, :, :head_width].reshape(row_cells, tables, head_count, DH)
    key_rows = projected[:, :, head_width : 2 * head_width]
    value_rows = projected[:, :, 2 * head_width :]
    offset = lax.axis_index("expert") * row_cells
    own_positions = offset + jnp.arange(row_cells, dtype=jnp.int32)
    start_state = (
        jnp.full((tables, head_count, row_cells), -1e30, jnp.float32),
        jnp.zeros((tables, head_count, row_cells), jnp.float32),
        jnp.zeros((tables, head_count, row_cells, DH), jnp.float32),
    )
    key_piece = lax.all_gather(key_rows, "expert", axis=0, tiled=True)
    value_piece = lax.all_gather(value_rows, "expert", axis=0, tiled=True)
    piece_len = key_piece.shape[0]
    block_len = math.gcd(piece_len, 512)
    block_count = piece_len // block_len
    key_blocks = key_piece.reshape(block_count, block_len, tables, head_count, DH)
    value_blocks = value_piece.reshape(block_count, block_len, tables, head_count, DH)
    block_starts = jnp.arange(block_count, dtype=jnp.int32) * block_len

    def step(carried, block_item):
        running_max, running_sum, accum = carried
        key_block, value_block, block_first = block_item
        scores = (
            jnp.einsum("qshd,kshd->shqk", queries, key_block, preferred_element_type=jnp.float32)
            * score_scale
        )
        key_valid = (block_first + jnp.arange(block_len, dtype=jnp.int32))[None, :] < lengths[
            :, None
        ]
        scores = jnp.where(key_valid[:, None, None, :], scores, -jnp.inf)
        new_max = jnp.maximum(running_max, jnp.max(scores, axis=-1))
        factor = jnp.exp(running_max - new_max)
        exp_scores = jnp.exp(scores - new_max[..., None])
        running_sum = running_sum * factor + jnp.sum(exp_scores, axis=-1)
        accum = accum * factor[..., None] + jnp.einsum(
            "shqk,kshd->shqd",
            exp_scores.astype(jnp.bfloat16),
            value_block,
            preferred_element_type=jnp.float32,
        )
        return ((new_max, running_sum, accum), None)

    finished, _ = lax.scan(step, start_state, (key_blocks, value_blocks, block_starts))
    running_max, running_sum, accum = finished
    normalized = accum / running_sum[..., None]
    live = own_positions[None, :] < lengths[:, None]
    normalized = jnp.where(live[:, None, :, None], normalized, 0.0)
    attended = (
        jnp.transpose(normalized, (2, 0, 1, 3))
        .reshape(row_cells, tables, head_width)
        .astype(jnp.bfloat16)
    )
    count_rows = cell_count * lax.axis_size("head")
    product = jnp.dot(
        attended.reshape(count_rows * tables, head_width), w_out, preferred_element_type=jnp.float32
    )
    summed = lax.psum_scatter(
        product.reshape(count_rows, tables, model_width).astype(jnp.bfloat16),
        "head",
        scatter_dimension=0,
        tiled=True,
    ).astype(jnp.float32)
    residual = table_cells.astype(jnp.float32) + summed
    mean_square = jnp.mean(residual * residual, axis=-1, keepdims=True)
    normed = (residual * lax.rsqrt(mean_square + 1e-06) * norm_gain.astype(jnp.float32)).astype(
        jnp.bfloat16
    )
    rows_dev = cell_count * tables
    normed_rows = normed.reshape(rows_dev, model_width)
    expert_count = lax.axis_size("expert") * lax.axis_size("head") // 2
    slot_cap = 2 * max(1, rows_dev // expert_count)
    target = expert_of_cell.reshape(rows_dev) * slot_cap + slot_of_cell.reshape(rows_dev)
    slot_table = (
        jnp.arange(expert_count * slot_cap, dtype=jnp.int32)[:, None] == target[None, :]
    ).astype(jnp.bfloat16)
    send_rows = jnp.dot(slot_table, normed_rows, preferred_element_type=jnp.float32).astype(
        jnp.bfloat16
    )
    gate_half = w_gate[0]
    up_half = w_up[0]
    down_half = w_down[0]
    split_rows = send_rows.reshape(2 * expert_count, slot_cap // 2, model_width)
    received = lax.all_to_all(
        split_rows, ("expert", "head"), split_axis=0, concat_axis=0, tiled=True
    )
    item_count = received.shape[1]
    partner_rows = from_partner(received, "head", 0)
    apply_received = jnp.concatenate([received, partner_rows], axis=1)
    sources = apply_received.shape[0]
    apply_item_count = apply_received.shape[1]
    flat_rows = apply_received.reshape(sources * apply_item_count, model_width)
    computed = expert_half(flat_rows, gate_half, up_half, down_half).reshape(
        sources, apply_item_count, model_width
    )
    returned = from_partner(computed[:, item_count:], "head", 0)
    merged = (computed[:, :item_count].astype(jnp.float32) + returned.astype(jnp.float32)).astype(
        jnp.bfloat16
    )
    gathered = lax.all_to_all(merged, ("expert", "head"), split_axis=0, concat_axis=0, tiled=True)
    combined = gathered.reshape(expert_count * slot_cap, model_width)
    expert_out = lax.dot_general(
        slot_table, combined, (((0,), (0,)), ((), ())), preferred_element_type=jnp.float32
    )
    updated = (residual.reshape(rows_dev, model_width) + expert_out).astype(jnp.bfloat16)
    return updated.reshape(cell_count, tables, model_width)


def solution(mesh):
    placed = (
        P(("expert", "head"), None, None),
        P(None, "head"),
        P(None, "head"),
        P(None, "head"),
        P("head", None),
        P(),
        P(("expert", "head"), None, None),
        P(("expert", "head"), None, None),
        P(("expert", "head"), None, None),
        P(),
        P(("expert", "head"), None),
        P(("expert", "head"), None),
    )
    pairs = mesh.shape["expert"] == 4 and mesh.shape["head"] == 8
    return jax.shard_map(
        paired_shards if pairs else shards,
        mesh=mesh,
        in_specs=placed,
        out_specs=P(("expert", "head"), None, None),
        check_vma=False,
    )
```
